32 devices in a mesh: dp: 4 (over z), mp: 8 (over y, x, core).
Axes of the slice: x: 2, y: 2, z: 4, core: 2. Of those that a mesh axis runs over, the one named last changes fastest.
Arguments:
- output_gradient: bfloat16 [3072, 8192], P('dp', 'mp'), may hold values from -6 to 6
- saved_gate_value: bfloat16 [3072, 14336], P('dp', 'mp'), may hold values from -6 to 6
- saved_up_value: bfloat16 [3072, 14336], P('dp', 'mp'), may hold values from -6 to 6
- down_weight: bfloat16 [14336, 8192], P('mp', 'dp'), may hold values from -0.046875 to 0.046875
- adapter_first_weight: bfloat16 [64, 64, 14336], P('dp', None, 'mp'), may hold values from -0.046875 to 0.046875
- adapter_second_weight: bfloat16 [64, 64, 8192], P('dp', None, 'mp'), may hold values from -0.0625 to 0.0625
- adapter_of_block: int32 [48], replicated, may hold values from 0 to 63, as said below
- slot_of_adapter: int32 [64], replicated, may hold values from 0 to 63, as said below
Outputs:
- d_gate: bfloat16 [3072, 14336], P('dp', 'mp')
- d_up: bfloat16 [3072, 14336], P('dp', 'mp')
- grad_a: float32 [64, 64, 14336], P('dp', None, 'mp')
- grad_b: float32 [64, 64, 8192], P('dp', None, 'mp')
The draws below stay inside these ranges and needn't reach their ends.
Inputs may be any that keep to these rules, and one draw needn't show every extreme that they name: `adapter_of_block`: block k holds tokens k * 64 to k * 64 + 63; group g holds blocks g * 12 onward. Slot s belongs to owner s // 16; the blocks of one group use adapters of any one owner at most 3 times, and in every draw one owner takes exactly 3 blocks of every group. A permutation: adapter a is stored at index slot_of_adapter[a] of adapter_first_weight, adapter_second_weight, grad_a and grad_b.
All inputs are finite; a program needn't handle non-finite values.
Results may differ from the reference program's by a relative error of at most 0.0057.
Values may be sent and summed in bfloat16 or wider, within the bound.
No kernel may reach another device: no remote copies, remote signals or barrier semaphores. Data moves between devices by JAX's collectives and lax.ppermute only.
A program may use at most 128 MiB of HBM per device.

```python
import jax
import jax.numpy as jnp

MODEL_WIDTH = 8192
HIDDEN_UNITS = 14336
ADAPTER_RANK = 64
ADAPTER_TOTAL = 64
BLK = 64
TOK_G = 768
TOKENS = 3072
CAP = 3
N_DP = 4


def layout_draw(key):
    root = jax.random.fold_in(key, 7001)
    slot_map = jax.random.permutation(jax.random.fold_in(root, 1), ADAPTER_TOTAL)
    per_group = TOK_G // BLK
    owner_totals = ADAPTER_TOTAL // N_DP
    hot_owner = jax.random.randint(jax.random.fold_in(root, 2), (), 0, N_DP)

    def one_group(group_key):
        others = jax.random.permutation(jax.random.fold_in(group_key, 1), N_DP - 1)
        owner_order = jnp.concatenate([hot_owner[None], (hot_owner + 1 + others) % N_DP])
        pool = jnp.repeat(owner_order, CAP)[:per_group]
        position = jax.random.permutation(jax.random.fold_in(group_key, 2), per_group)
        owner_of = pool[position]
        choose = jax.random.randint(jax.random.fold_in(group_key, 3), (per_group,), 0, owner_totals)
        return owner_of * owner_totals + choose
    group_keys = jax.random.split(jax.random.fold_in(root, 3), N_DP)
    slots = jax.vmap(one_group)(group_keys).reshape(-1)
    inverse = jnp.argsort(slot_map)
    return (inverse[slots].astype(jnp.int32), slot_map.astype(jnp.int32))


def draw_adapter_of_block(key, part):
    return layout_draw(key)[0]


def draw_slot_of_adapter(key, part):
    return layout_draw(key)[1]


def levels(own_key, shape, pieces, smallest, largest):
    gain = 1.0
    for dim, blocks in pieces:
        steps = jax.random.uniform(jax.random.fold_in(jax.random.fold_in(own_key, 6), dim), (blocks,), jnp.float32, smallest / len(pieces), largest / len(pieces))
        gain = gain * jnp.repeat(jnp.exp(steps), shape[dim] // blocks).reshape((-1,) + (1,) * (len(shape) - 1 - dim))
    return gain


def normal_values(rng, dims, deviation, limit, cuts=(), dtype=jnp.bfloat16):
    factor_of = levels(rng, dims, cuts, -0.22, 0.18) if cuts else 1.0
    result = jax.random.normal(rng, dims, jnp.float32) * deviation * factor_of
    return jnp.minimum(jnp.maximum(result, -limit), limit).astype(dtype)


def setup_inputs(seed: int = 0) -> dict:
    streams_of = jax.random.split(jax.random.key(seed), 9)
    output_gradient = normal_values(streams_of[0], (TOKENS, MODEL_WIDTH), 1.0, 6.0, ((0, 4), (1, 8)))
    saved_gate_value = normal_values(streams_of[1], (TOKENS, HIDDEN_UNITS), 1.0, 6.0, ((0, 4), (1, 8)))
    saved_up_value = normal_values(streams_of[2], (TOKENS, HIDDEN_UNITS), 1.0, 6.0, ((0, 4), (1, 8)))
    down_weight = normal_values(streams_of[3], (HIDDEN_UNITS, MODEL_WIDTH), HIDDEN_UNITS ** -0.5, 0.046875, ((0, 8), (1, 4)))
    adapter_first_weight = normal_values(streams_of[4], (ADAPTER_TOTAL, ADAPTER_RANK, HIDDEN_UNITS), HIDDEN_UNITS ** -0.5, 0.046875, ((0, 4), (2, 8)))
    adapter_second_weight = normal_values(streams_of[5], (ADAPTER_TOTAL, ADAPTER_RANK, MODEL_WIDTH), MODEL_WIDTH ** -0.5, 0.0625, ((0, 4), (2, 8)))
    adapter_of_block = draw_adapter_of_block(jax.random.fold_in(streams_of[8], 71), 0)
    slot_of_adapter = draw_slot_of_adapter(jax.random.fold_in(streams_of[8], 71), 0)
    return {"output_gradient": output_gradient, "saved_gate_value": saved_gate_value, "saved_up_value": saved_up_value, "down_weight": down_weight, "adapter_first_weight": adapter_first_weight, "adapter_second_weight": adapter_second_weight, "adapter_of_block": adapter_of_block, "slot_of_adapter": slot_of_adapter}


adapter_scale = 2.0


def reference(output_gradient, saved_gate_value, saved_up_value, down_weight, adapter_first_weight, adapter_second_weight, adapter_of_block, slot_of_adapter):
    gate_float = saved_gate_value.astype(jnp.float32)
    up_float = saved_up_value.astype(jnp.float32)
    squash = jax.nn.sigmoid(gate_float)
    activated = gate_float * squash
    hidden = (activated * up_float).astype(jnp.bfloat16)
    block_count = adapter_of_block.shape[0]
    slot_of_block = slot_of_adapter[adapter_of_block]
    hidden_blocks = hidden.reshape(block_count, BLK, hidden.shape[1]).astype(jnp.float32)
    output_blocks = output_gradient.reshape(block_count, BLK, output_gradient.shape[1]).astype(jnp.float32)
    first_factor_blocks = adapter_first_weight[slot_of_block].astype(jnp.float32)
    second_factor_blocks = adapter_second_weight[slot_of_block].astype(jnp.float32)
    downward_factor = jnp.einsum('ntf,nrf->ntr', hidden_blocks, first_factor_blocks).astype(jnp.bfloat16)
    backward_factor = (adapter_scale * jnp.einsum('ysx,ykx->ysk', output_blocks, second_factor_blocks)).astype(jnp.bfloat16)
    side_term = jnp.einsum('ntr,nrf->ntf', backward_factor.astype(jnp.float32), first_factor_blocks).reshape(hidden.shape)
    base_term = jnp.dot(output_gradient, down_weight.T, preferred_element_type=jnp.float32)
    d_hidden = base_term + side_term
    d_gate = (d_hidden * up_float * squash * (1.0 + gate_float * (1.0 - squash))).astype(jnp.bfloat16)
    d_up = (d_hidden * activated).astype(jnp.bfloat16)
    piece_a = jnp.einsum('ntr,ntf->nrf', backward_factor.astype(jnp.float32), hidden_blocks).astype(jnp.bfloat16)
    second_factor_piece = (adapter_scale * jnp.einsum('cxh,cxe->che', downward_factor.astype(jnp.float32), output_blocks)).astype(jnp.bfloat16)
    grad_a = jax.ops.segment_sum(piece_a.astype(jnp.float32), slot_of_block, num_segments=ADAPTER_TOTAL)
    grad_b = jax.ops.segment_sum(second_factor_piece.astype(jnp.float32), slot_of_block, num_segments=ADAPTER_TOTAL)
    return d_gate, d_up, grad_a, grad_b
```

```python
import jax
import jax.numpy as jnp
from jax import lax
from jax.sharding import PartitionSpec as P

ADAPTER_RANK = 64
BLK = 64


adapter_scale = 2.0


def sum_over_mp(x):
    size = lax.axis_size("mp")
    if size & (size - 1):
        return lax.psum(x, "mp")
    bit = 1
    while bit < size:
        x = x + lax.ppermute(x, "mp", [(i, i ^ bit) for i in range(size)])
        bit *= 2
    return x


def gather_over_mp(x):
    size = lax.axis_size("mp")
    if size != 8:
        return lax.all_gather(x, "mp", axis=0)

    def swap(v, bits):
        return lax.ppermute(v, "mp", [(i, i ^ bits) for i in range(size)])

    half = x.shape[0] // 2
    x1 = swap(x, 1)
    x2, x4 = swap(x, 2), swap(x, 4)
    x6 = jnp.concatenate([swap(x4[:half], 2), swap(x2[half:], 4)])
    x3, x5 = swap(x2, 1), swap(x4, 1)
    x7 = swap(x6, 1)
    return jnp.take(
        jnp.stack([x, x1, x2, x3, x4, x5, x6, x7]),
        jnp.arange(size, dtype=jnp.int32) ^ lax.axis_index("mp"),
        axis=0,
    )


def pick(values, table, my_group):
    places = sorted(set(table))
    result = values[places[0]]
    mine = jnp.asarray(table, jnp.int32)[jnp.minimum(my_group, len(table) - 1)]
    for place in places[1:]:
        result = jnp.where(mine == place, values[place], result)
    return result


def shards(
    output_gradient,
    saved_gate_value,
    saved_up_value,
    down_weight,
    adapter_first_weight,
    adapter_second_weight,
    adapter_of_block,
    slot_of_adapter,
):
    groups = lax.axis_size("dp")
    members = lax.axis_size("mp")
    my_group = lax.axis_index("dp")
    tok_rows = output_gradient.shape[0]
    blocks = tok_rows // BLK
    owner_totals = adapter_first_weight.shape[0]
    adapters = slot_of_adapter.shape[0]
    ff_local = saved_gate_value.shape[1]
    d_local = output_gradient.shape[1]
    slice_width = down_weight.shape[1]
    capacity = (blocks + groups - 1) // groups

    match_table = adapter_of_block[:, None] == jnp.arange(adapters, dtype=jnp.int32)[None, :]
    slot_of_block = jnp.sum(jnp.where(match_table, slot_of_adapter[None, :], 0), axis=1)
    owners = (slot_of_block // owner_totals).reshape(groups, blocks)
    local_slot = (slot_of_block % owner_totals).reshape(groups, blocks)
    block_index = jnp.arange(blocks, dtype=jnp.int32)
    earlier = (owners[:, :, None] == owners[:, None, :]) & (
        block_index[None, None, :] < block_index[None, :, None]
    )
    ranks = jnp.sum(earlier.astype(jnp.int32), axis=2)
    rank_values = jnp.arange(capacity, dtype=jnp.int32)
    hits = (owners == my_group)[:, None, :] & (ranks[:, None, :] == rank_values[None, :, None])
    incoming_valid = jnp.any(hits, axis=2)
    arriving_slot = jnp.sum(jnp.where(hits, local_slot[:, None, :], 0), axis=2)
    own_owner = lax.dynamic_index_in_dim(owners, my_group, 0, keepdims=False)
    own_rank = lax.dynamic_index_in_dim(ranks, my_group, 0, keepdims=False)
    group_values = jnp.arange(groups, dtype=jnp.int32)
    route_table = (own_owner[None, None, :] == group_values[:, None, None]) & (
        own_rank[None, None, :] == rank_values[None, :, None]
    )
    route_valid = jnp.any(route_table, axis=2)
    route_block = jnp.sum(jnp.where(route_table, block_index[None, None, :], 0), axis=2)

    def to_owners(rows):
        sent = jnp.where(
            route_valid[:, :, None, None],
            jnp.take(rows.reshape(blocks, BLK, rows.shape[1]), route_block, axis=0),
            jnp.zeros((), rows.dtype),
        )
        return lax.all_to_all(sent, "dp", split_axis=0, concat_axis=0, tiled=True)

    recv_o = to_owners(output_gradient)
    share = tok_rows // members
    by_tokens = lax.all_to_all(
        output_gradient.reshape(members, share, d_local), "mp", split_axis=0, concat_axis=0, tiled=True
    )
    by_tokens = by_tokens.transpose(1, 0, 2).reshape(share, groups, slice_width).transpose(1, 0, 2)
    by_slice = lax.all_to_all(by_tokens, "dp", split_axis=0, concat_axis=0, tiled=True)
    out_slices = gather_over_mp(by_slice)

    gate_float = saved_gate_value.astype(jnp.float32)
    up_float = saved_up_value.astype(jnp.float32)
    squash = jax.nn.sigmoid(gate_float)
    activated = gate_float * squash
    hidden = (activated * up_float).astype(jnp.bfloat16)
    recv_h = to_owners(hidden)

    a_here = jnp.take(adapter_first_weight, arriving_slot, axis=0)
    b_here = jnp.take(adapter_second_weight, arriving_slot, axis=0)
    back_factor = (
        adapter_scale
        * sum_over_mp(
            jnp.einsum("gctd,gcrd->gctr", recv_o, b_here, preferred_element_type=jnp.float32)
        )
    ).astype(jnp.bfloat16)
    down_factor = sum_over_mp(
        jnp.einsum("gctf,gcrf->gctr", recv_h, a_here, preferred_element_type=jnp.float32)
    ).astype(jnp.bfloat16)

    spread = jnp.where(
        hits.transpose(0, 2, 1)[:, :, None, :, None],
        back_factor.transpose(0, 2, 1, 3)[:, None],
        jnp.zeros((), jnp.bfloat16),
    ).reshape(groups, tok_rows, capacity * ADAPTER_RANK)
    a_rows = a_here.reshape(groups, capacity * ADAPTER_RANK, ff_local)
    order = [
        sorted(range(groups), key=lambda target: (-abs(target - i), -target)) for i in range(groups)
    ]
    place = [[order[i].index(target) for target in range(groups)] for i in range(groups)]
    order_here = jnp.asarray(order, jnp.int32)[my_group]
    partial = []
    for k in range(groups):
        target = order_here[k]
        rows = lax.dynamic_index_in_dim(out_slices, target, 1, keepdims=False).reshape(
            tok_rows, slice_width
        )
        base = lax.dot_general(
            rows, down_weight, (((1,), (1,)), ((), ())), preferred_element_type=jnp.float32
        )
        side = jnp.dot(
            lax.dynamic_index_in_dim(spread, target, 0, keepdims=False),
            lax.dynamic_index_in_dim(a_rows, target, 0, keepdims=False),
            preferred_element_type=jnp.float32,
        )
        partial.append((base + side).astype(jnp.bfloat16))

    from_left = from_right = None
    for step in range(1, groups):
        reach = groups - step
        send_r = pick(partial, [place[i][i + reach] for i in range(step)], my_group)
        send_l = pick(
            partial,
            [place[groups - 1 - i][groups - 1 - i - reach] for i in range(step)],
            groups - 1 - my_group,
        )
        if from_left is not None:
            send_r = (send_r.astype(jnp.float32) + from_left.astype(jnp.float32)).astype(jnp.bfloat16)
            send_l = (send_l.astype(jnp.float32) + from_right.astype(jnp.float32)).astype(jnp.bfloat16)
        from_left = lax.ppermute(send_r, "dp", [(i, i + 1) for i in range(step)])
        from_right = lax.ppermute(
            send_l, "dp", [(groups - 1 - i, groups - 2 - i) for i in range(step)]
        )
    d_hidden = partial[groups - 1].astype(jnp.float32)
    if from_left is not None:
        d_hidden = d_hidden + from_left.astype(jnp.float32) + from_right.astype(jnp.float32)
    d_gate = (d_hidden * up_float * squash * (1.0 + gate_float * (1.0 - squash))).astype(
        jnp.bfloat16
    )
    d_up = (d_hidden * activated).astype(jnp.bfloat16)

    terms_a = jnp.einsum(
        "gctr,gctf->gcrf", back_factor, recv_h, preferred_element_type=jnp.float32
    ).astype(jnp.bfloat16)
    terms_b = (
        adapter_scale
        * jnp.einsum("gctr,gctd->gcrd", down_factor, recv_o, preferred_element_type=jnp.float32)
    ).astype(jnp.bfloat16)
    flat_slot = arriving_slot.reshape(groups * capacity)
    flat_valid = incoming_valid.reshape(groups * capacity)
    selector = (
        (flat_slot[None, :] == jnp.arange(owner_totals, dtype=jnp.int32)[:, None])
        & flat_valid[None, :]
    ).astype(jnp.bfloat16)
    grad_a = jnp.dot(
        selector,
        terms_a.reshape(groups * capacity, ADAPTER_RANK * ff_local),
        preferred_element_type=jnp.float32,
    ).reshape(owner_totals, ADAPTER_RANK, ff_local)
    grad_b = jnp.dot(
        selector,
        terms_b.reshape(groups * capacity, ADAPTER_RANK * d_local),
        preferred_element_type=jnp.float32,
    ).reshape(owner_totals, ADAPTER_RANK, d_local)
    return (d_gate, d_up, grad_a, grad_b)


def solution(mesh):
    in_specs = (
        P("dp", "mp"),
        P("dp", "mp"),
        P("dp", "mp"),
        P("mp", "dp"),
        P("dp", None, "mp"),
        P("dp", None, "mp"),
        P(),
        P(),
    )
    out_specs = (P("dp", "mp"), P("dp", "mp"), P("dp", None, "mp"), P("dp", None, "mp"))
    return jax.shard_map(shards, mesh=mesh, in_specs=in_specs, out_specs=out_specs, check_vma=False)
```

```python
import functools

import jax
import jax.numpy as jnp
from jax import lax
from jax.experimental import pallas as pl
from jax.experimental.pallas import tpu as pltpu
from jax.sharding import PartitionSpec as P

ADAPTER_RANK = 64
BLK = 64
VMEM_BYTES = 48 * 1024 * 1024


adapter_scale = 2.0


def sum_over_mp(x):
    size = lax.axis_size("mp")
    if size & (size - 1):
        return lax.psum(x, "mp")
    bit = 1
    while bit < size:
        x = x + lax.ppermute(x, "mp", [(i, i ^ bit) for i in range(size)])
        bit *= 2
    return x


def exchange_over_dp(parts):
    size = lax.axis_size("dp")
    me = lax.axis_index("dp")
    if size > 4:
        return lax.all_to_all(parts, "dp", split_axis=0, concat_axis=0, tiled=True)
    got = [lax.dynamic_index_in_dim(parts, me, 0, keepdims=False)]
    for shift in range(1, size):
        sent = lax.dynamic_index_in_dim(parts, (me + shift) % size, 0, keepdims=False)
        got.append(lax.ppermute(sent, "dp", [(i, (i + shift) % size) for i in range(size)]))
    index = (me - jnp.arange(size, dtype=jnp.int32)) % size
    return jnp.take(jnp.stack(got), index, axis=0)


def slices_to_planes(out, groups, members):
    tok_rows, d_local = out.shape
    share = tok_rows // members
    me = lax.axis_index("mp")
    my_group = lax.axis_index("dp")
    if members % groups or members > 8:
        moved = lax.all_to_all(
            out.reshape(members, share, d_local), "mp", split_axis=0, concat_axis=0, tiled=True
        )
        moved = moved.transpose(1, 0, 2).reshape(share, groups, -1).transpose(1, 0, 2)
        return lax.all_to_all(moved, "dp", split_axis=0, concat_axis=0, tiled=True)
    per = members // groups
    got = []
    chunks = out.reshape(members, share, d_local)
    for turn in range(members):
        pairs = []
        for g in range(groups):
            for m in range(members):
                to = (g * per + m % per + turn) % members
                pairs.append((g * members + m, (m // per) * members + to))
        to = (my_group * per + me % per + turn) % members
        sent = lax.dynamic_index_in_dim(chunks, to, 0, keepdims=False)
        got.append(lax.ppermute(sent, ("dp", "mp"), pairs))
    index = (me - jnp.arange(members, dtype=jnp.int32)) % members
    ordered = jnp.take(jnp.stack(got), index, axis=0)
    return (
        ordered.reshape(groups, per, share, d_local)
        .transpose(0, 2, 1, 3)
        .reshape(groups, share, per * d_local)
    )


def gather_over_mp(x):
    size = lax.axis_size("mp")
    me = lax.axis_index("mp")
    groups, share, width = x.shape
    if size != 8 or share % 32:
        whole = lax.all_gather(x, "mp", axis=1, tiled=True)
        return [whole], [jnp.zeros((), jnp.int32)]

    def swap(v, bits):
        return lax.ppermute(v, "mp", [(i, i ^ bits) for i in range(size)])

    half = share // 2
    x2, x4 = swap(x, 2), swap(x, 4)
    x1 = swap(x, 1)
    x6a, x6b = swap(x4[:, :half], 2), swap(x2[:, half:], 4)
    x3, x5 = swap(x2, 1), swap(x4, 1)
    x7a, x7b = swap(x6a, 1), swap(x6b, 1)
    pieces = [x, x1, x2, x3, x4, x5, x6a, x6b, x7a, x7b]
    owners = [0, 1, 2, 3, 4, 5, 6, 6, 7, 7]
    extra = [0, 0, 0, 0, 0, 0, 0, half, 0, half]
    return pieces, [(me ^ k) * share + e for k, e in zip(owners, extra)]


def partial_kernel(count, aligned, info, *refs):
    pieces, (w_ref, s_ref, a_ref), outs, rows_ref = (
        refs[:count],
        refs[count : count + 3],
        refs[count + 3 : -1],
        refs[-1],
    )

    @pl.when(pl.program_id(0) == 0)
    def _():
        for k, piece in enumerate(pieces):
            rows = piece.shape[1]
            if count == 1:
                rows_ref[...] = piece[0]
            else:
                start = pl.multiple_of(info[1 + k], aligned)
                rows_ref[pl.ds(start, rows), :] = piece[0]

    half = outs[0].shape[0]
    for h, out in enumerate(outs):
        span = slice(h * half, (h + 1) * half)
        total = lax.dot_general(
            rows_ref[span, :], w_ref[...], (((1,), (1,)), ((), ())), preferred_element_type=jnp.float32
        )
        total += jnp.dot(s_ref[0, span, :], a_ref[0], preferred_element_type=jnp.float32)
        out[...] = total.astype(out.dtype)


def partial_sums(target, pieces, starts, weight, spread, a_rows, halves, dtype):
    ff_local, width = weight.shape
    tok_rows, side = spread.shape[1:]
    tile = 256 if ff_local % 256 == 0 else ff_local
    info = jnp.stack([target, *starts]).astype(jnp.int32)
    aligned = functools.reduce(
        lambda a, b: a if b % a == 0 else 16, [p.shape[1] for p in pieces], 16
    )
    return pl.pallas_call(
        functools.partial(partial_kernel, len(pieces), aligned),
        grid_spec=pltpu.PrefetchScalarGridSpec(
            num_scalar_prefetch=1,
            grid=(ff_local // tile,),
            in_specs=[
                pl.BlockSpec((1, p.shape[1], width), lambda n, info: (info[0], 0, 0)) for p in pieces
            ]
            + [
                pl.BlockSpec((tile, width), lambda n, info: (n, 0)),
                pl.BlockSpec((1, tok_rows, side), lambda n, info: (info[0], 0, 0)),
                pl.BlockSpec((1, side, tile), lambda n, info: (info[0], 0, n)),
            ],
            out_specs=[
                pl.BlockSpec((tok_rows // halves, tile), lambda n, info: (0, n))
                for _ in range(halves)
            ],
            scratch_shapes=[pltpu.VMEM((tok_rows, width), jnp.bfloat16)],
        ),
        out_shape=[
            jax.ShapeDtypeStruct((tok_rows // halves, ff_local), dtype) for _ in range(halves)
        ],
        compiler_params=pltpu.CompilerParams(vmem_limit_bytes=VMEM_BYTES),
        name="partial_sums",
    )(info, *pieces, weight, spread, a_rows)


def finish_kernel(own, left, right, gate, up, *rest):
    d_gate, d_up = rest[-2:]
    d_hidden = own[...] + left[...].astype(jnp.float32) + right[...].astype(jnp.float32)
    gate_float = gate[...].astype(jnp.float32)
    up_float = up[...].astype(jnp.float32)
    squash = jax.nn.sigmoid(gate_float)
    d_gate[...] = (d_hidden * up_float * squash * (1.0 + gate_float * (1.0 - squash))).astype(
        d_gate.dtype
    )
    d_up[...] = (d_hidden * (gate_float * squash)).astype(d_up.dtype)


def finish(own, left, right, gate, up, part, earlier):
    rows, ff_local = own.shape
    step = 64 if rows % 64 == 0 else rows
    steps = rows // step
    here = pl.BlockSpec((step, ff_local), lambda i: (i, 0))
    there = pl.BlockSpec((step, ff_local), lambda i: (part * steps + i, 0))
    before = [] if earlier is None else list(earlier)
    return pl.pallas_call(
        finish_kernel,
        grid=(steps,),
        in_specs=[here, here, here, there, there] + [pl.BlockSpec(memory_space=pl.ANY)] * len(before),
        out_specs=[there, there],
        out_shape=[jax.ShapeDtypeStruct(gate.shape, gate.dtype) for _ in range(2)],
        input_output_aliases={5: 0, 6: 1} if before else {},
        compiler_params=pltpu.CompilerParams(vmem_limit_bytes=VMEM_BYTES),
        name="finish",
    )(own, left, right, gate, up, *before)


def shards(
    output_gradient,
    saved_gate_value,
    saved_up_value,
    down_weight,
    adapter_first_weight,
    adapter_second_weight,
    adapter_of_block,
    slot_of_adapter,
):
    groups = lax.axis_size("dp")
    members = lax.axis_size("mp")
    my_group = lax.axis_index("dp")
    tok_rows = output_gradient.shape[0]
    blocks = tok_rows // BLK
    owner_totals = adapter_first_weight.shape[0]
    adapters = slot_of_adapter.shape[0]
    ff_local = saved_gate_value.shape[1]
    d_local = output_gradient.shape[1]
    capacity = (blocks + groups - 1) // groups
    halves = 2

    by_slice = slices_to_planes(output_gradient, groups, members)
    pieces, starts = gather_over_mp(by_slice)

    match_table = adapter_of_block[:, None] == jnp.arange(adapters, dtype=jnp.int32)[None, :]
    slot_of_block = jnp.sum(jnp.where(match_table, slot_of_adapter[None, :], 0), axis=1)
    owners = (slot_of_block // owner_totals).reshape(groups, blocks)
    local_slot = (slot_of_block % owner_totals).reshape(groups, blocks)
    block_index = jnp.arange(blocks, dtype=jnp.int32)
    earlier = (owners[:, :, None] == owners[:, None, :]) & (
        block_index[None, None, :] < block_index[None, :, None]
    )
    ranks = jnp.sum(earlier.astype(jnp.int32), axis=2)
    rank_values = jnp.arange(capacity, dtype=jnp.int32)
    hits = (owners == my_group)[:, None, :] & (ranks[:, None, :] == rank_values[None, :, None])
    incoming_valid = jnp.any(hits, axis=2)
    arriving_slot = jnp.sum(jnp.where(hits, local_slot[:, None, :], 0), axis=2)
    own_owner = lax.dynamic_index_in_dim(owners, my_group, 0, keepdims=False)
    own_rank = lax.dynamic_index_in_dim(ranks, my_group, 0, keepdims=False)
    group_values = jnp.arange(groups, dtype=jnp.int32)
    route_table = (own_owner[None, None, :] == group_values[:, None, None]) & (
        own_rank[None, None, :] == rank_values[None, :, None]
    )
    route_valid = jnp.any(route_table, axis=2)
    route_block = jnp.sum(jnp.where(route_table, block_index[None, None, :], 0), axis=2)

    def to_owners(rows):
        sent = jnp.where(
            route_valid[:, :, None, None],
            jnp.take(rows.reshape(blocks, BLK, rows.shape[1]), route_block, axis=0),
            jnp.zeros((), rows.dtype),
        )
        return exchange_over_dp(sent)

    recv_o = to_owners(output_gradient)
    gate_float = saved_gate_value.astype(jnp.float32)
    hidden = (
        gate_float * jax.nn.sigmoid(gate_float) * saved_up_value.astype(jnp.float32)
    ).astype(jnp.bfloat16)
    recv_h = to_owners(hidden)

    a_here = jnp.take(adapter_first_weight, arriving_slot, axis=0)
    b_here = jnp.take(adapter_second_weight, arriving_slot, axis=0)
    back_factor = (
        adapter_scale
        * sum_over_mp(
            jnp.einsum("gctd,gcrd->gctr", recv_o, b_here, preferred_element_type=jnp.float32)
        )
    ).astype(jnp.bfloat16)
    down_factor = sum_over_mp(
        jnp.einsum("gctf,gcrf->gctr", recv_h, a_here, preferred_element_type=jnp.float32)
    ).astype(jnp.bfloat16)

    spread = jnp.where(
        hits.transpose(0, 2, 1)[:, :, None, :, None],
        back_factor.transpose(0, 2, 1, 3)[:, None],
        jnp.zeros((), jnp.bfloat16),
    ).reshape(groups, tok_rows, capacity * ADAPTER_RANK)
    a_rows = a_here.reshape(groups, capacity * ADAPTER_RANK, ff_local)

    def partial_for(target, dtype=jnp.bfloat16):
        return partial_sums(
            target, pieces, starts, down_weight, spread, a_rows, halves, dtype
        )

    def joined(a, *more):
        total = a.astype(jnp.float32)
        for m in more:
            total = total + m.astype(jnp.float32)
        return total.astype(jnp.bfloat16)

    last = groups - 1
    nothing = [jnp.zeros((tok_rows // halves, ff_local), jnp.bfloat16)] * halves
    from_left, from_right = nothing, nothing
    for step in range(1, groups):
        reach = groups - step
        to_right = jnp.where(my_group + reach <= last, my_group + reach, 0)
        to_left = jnp.where(my_group >= reach, my_group - reach, 0)
        pairs_r = [(i, i + 1) for i in range(step)]
        pairs_l = [(last - i, last - 1 - i) for i in range(step)]
        if step <= reach:
            part = partial_for(jnp.where(my_group + reach <= last, to_right, to_left))
            if step > 1:
                part = [joined(p, a, b) for p, a, b in zip(part, from_left, from_right)]
            send_r = send_l = part
        else:
            send_r = [joined(p, a) for p, a in zip(partial_for(to_right), from_left)]
            send_l = [joined(p, a) for p, a in zip(partial_for(to_left), from_right)]
        from_left = [lax.ppermute(s, "dp", pairs_r) for s in send_r]
        from_right = [lax.ppermute(s, "dp", pairs_l) for s in send_l]
    own = partial_for(my_group, jnp.float32)
    done = None
    for h in range(halves):
        done = finish(
            own[h], from_left[h], from_right[h], saved_gate_value, saved_up_value, h, done
        )
    d_gate, d_up = done

    terms_a = jnp.einsum(
        "gctr,gctf->gcrf", back_factor, recv_h, preferred_element_type=jnp.float32
    ).astype(jnp.bfloat16)
    terms_b = (
        adapter_scale
        * jnp.einsum("gctr,gctd->gcrd", down_factor, recv_o, preferred_element_type=jnp.float32)
    ).astype(jnp.bfloat16)
    flat_slot = arriving_slot.reshape(groups * capacity)
    flat_valid = incoming_valid.reshape(groups * capacity)
    selector = (
        (flat_slot[None, :] == jnp.arange(owner_totals, dtype=jnp.int32)[:, None])
        & flat_valid[None, :]
    ).astype(jnp.bfloat16)
    grad_a = jnp.dot(
        selector,
        terms_a.reshape(groups * capacity, ADAPTER_RANK * ff_local),
        preferred_element_type=jnp.float32,
    ).reshape(owner_totals, ADAPTER_RANK, ff_local)
    grad_b = jnp.dot(
        selector,
        terms_b.reshape(groups * capacity, ADAPTER_RANK * d_local),
        preferred_element_type=jnp.float32,
    ).reshape(owner_totals, ADAPTER_RANK, d_local)
    return (d_gate, d_up, grad_a, grad_b)


def solution(mesh):
    in_specs = (
        P("dp", "mp"),
        P("dp", "mp"),
        P("dp", "mp"),
        P("mp", "dp"),
        P("dp", None, "mp"),
        P("dp", None, "mp"),
        P(),
        P(),
    )
    out_specs = (P("dp", "mp"), P("dp", "mp"), P("dp", None, "mp"), P("dp", None, "mp"))
    return jax.shard_map(shards, mesh=mesh, in_specs=in_specs, out_specs=out_specs, check_vma=False)
```

```python
import functools

import jax
import jax.numpy as jnp
from jax import lax
from jax.experimental import pallas as pl
from jax.experimental.pallas import tpu as pltpu
from jax.sharding import PartitionSpec as P

ADAPTER_RANK = 64
BLK = 64
VMEM_BYTES = 48 * 1024 * 1024


adapter_scale = 2.0


def sum_over_mp(x):
    size = lax.axis_size("mp")
    if size & (size - 1):
        return lax.psum(x, "mp")
    bit = 1
    while bit < size:
        x = x + lax.ppermute(x, "mp", [(i, i ^ bit) for i in range(size)])
        bit *= 2
    return x


def pack_kernel(count, capacity, info, *refs):
    sources, packets = refs[:-count], refs[-count:]
    step = pl.program_id(0)
    if len(sources) == capacity:
        values = [source[...] for source in sources]
    else:
        values = []
        for c in range(capacity):
            gate = sources[c][...].astype(jnp.float32)
            up = sources[capacity + c][...].astype(jnp.float32)
            values.append((gate * jax.nn.sigmoid(gate) * up).astype(jnp.bfloat16))
    for j in range(count):

        @pl.when(step == j)
        def _():
            for c in range(capacity):
                packets[j][c * BLK : (c + 1) * BLK, :] = values[c]


def pack(route, *sources):
    count, capacity = route.shape
    width = sources[0].shape[1]
    spec = [
        pl.BlockSpec((BLK, width), lambda i, info, c=c: (info[i * capacity + c], 0))
        for c in range(capacity)
    ]
    packets = pl.pallas_call(
        functools.partial(pack_kernel, count, capacity),
        grid_spec=pltpu.PrefetchScalarGridSpec(
            num_scalar_prefetch=1,
            grid=(count,),
            in_specs=spec * len(sources),
            out_specs=[
                pl.BlockSpec((capacity * BLK, width), lambda i, info: (0, 0)) for _ in range(count)
            ],
        ),
        out_shape=[jax.ShapeDtypeStruct((capacity * BLK, width), sources[0].dtype)] * count,
        compiler_params=pltpu.CompilerParams(vmem_limit_bytes=VMEM_BYTES),
        name="pack",
    )(route.reshape(-1), *[s for s in sources for _ in range(capacity)])
    return list(packets)


def all_to_all_of(parts):
    got = lax.all_to_all(jnp.stack(parts), "dp", split_axis=0, concat_axis=0, tiled=True)
    return [got[g] for g in range(len(parts))]


def swap_over_dp(x, bits, only=None):
    size = lax.axis_size("dp")
    return lax.ppermute(x, "dp", [(i, i ^ bits) for i in range(size) if only is None or i in only])


def factor_kernel(capacity, slots, *refs):
    weights, packets, result = refs[:capacity], refs[capacity:-1], refs[-1]
    step = pl.program_id(0)
    for j, packet in enumerate(packets):

        @pl.when(step == j)
        def _():
            for c in range(capacity):
                result[c] = lax.dot_general(
                    packet[c * BLK : (c + 1) * BLK, :],
                    weights[c][0],
                    (((1,), (1,)), ((), ())),
                    preferred_element_type=jnp.float32,
                )


def factor_parts(packets, weight, slots):
    count, capacity = slots.shape
    rank, width = weight.shape[1:]
    return pl.pallas_call(
        functools.partial(factor_kernel, capacity),
        grid_spec=pltpu.PrefetchScalarGridSpec(
            num_scalar_prefetch=1,
            grid=(count,),
            in_specs=[
                pl.BlockSpec((1, rank, width), lambda i, slots, c=c: (slots[i * capacity + c], 0, 0))
                for c in range(capacity)
            ]
            + [pl.BlockSpec((capacity * BLK, width), lambda i, slots: (0, 0)) for _ in packets],
            out_specs=pl.BlockSpec((capacity, BLK, rank), lambda i, slots: (i, 0, 0)),
        ),
        out_shape=jax.ShapeDtypeStruct((count * capacity, BLK, rank), jnp.float32),
        compiler_params=pltpu.CompilerParams(vmem_limit_bytes=VMEM_BYTES),
        name="factor_parts",
    )(slots.reshape(-1), *[weight] * capacity, *packets)


def slices_of_tokens(out, groups, members, block_rows):
    tok_rows, d_local = out.shape
    share = tok_rows // members
    moved = lax.all_to_all(
        out.reshape(members, share, d_local), "mp", split_axis=0, concat_axis=0, tiled=True
    )
    if members % groups or share % 16 or groups != 4 or tok_rows // groups != block_rows:
        moved = moved.transpose(1, 0, 2).reshape(share, groups, -1).transpose(1, 0, 2)
        return moved[:, None], False
    return moved.reshape(groups, members // groups, share, d_local), True


def partial_kernel(capacity, info, units_ref, w_ref, factor_ref, *rest):
    a_refs, outs, rows_ref, total_ref = rest[:capacity], rest[capacity:-2], rest[-2], rest[-1]

    @pl.when(pl.program_id(0) == 0)
    def _():
        members, _, parts, rows, columns = units_ref.shape
        for m in range(members):
            for q in range(parts):
                rows_ref[m * rows : (m + 1) * rows, q * columns : (q + 1) * columns] = units_ref[
                    m, 0, q
                ]

    total_ref[...] = lax.dot_general(
        rows_ref[...], w_ref[...], (((1,), (1,)), ((), ())), preferred_element_type=jnp.float32
    )
    for c in range(capacity):

        @pl.when(info[2 + 3 * c] > 0)
        def _():
            rows = pl.ds(pl.multiple_of(info[3 + 3 * c] * BLK, BLK), BLK)
            total_ref[rows, :] += jnp.dot(
                factor_ref[0, c], a_refs[c][0], preferred_element_type=jnp.float32
            )

    half = outs[0].shape[0]
    for h, out in enumerate(outs):
        out[...] = total_ref[h * half : (h + 1) * half, :].astype(out.dtype)


def partial_sums(info, units, weight, factors, first, tok_rows, halves, dtype):
    ff_local, width = weight.shape
    capacity, _, rank = factors.shape[1:]
    tile = 256 if ff_local % 256 == 0 else ff_local
    members, _, parts, rows, columns = units.shape
    return pl.pallas_call(
        functools.partial(partial_kernel, capacity),
        grid_spec=pltpu.PrefetchScalarGridSpec(
            num_scalar_prefetch=1,
            grid=(ff_local // tile,),
            in_specs=[
                pl.BlockSpec(
                    (members, 1, parts, rows, columns), lambda n, info: (0, info[0], 0, 0, 0)
                ),
                pl.BlockSpec((tile, width), lambda n, info: (n, 0)),
                pl.BlockSpec((1, capacity, BLK, rank), lambda n, info: (info[1], 0, 0, 0)),
            ]
            + [
                pl.BlockSpec((1, rank, tile), lambda n, info, c=c: (info[4 + 3 * c], 0, n))
                for c in range(capacity)
            ],
            out_specs=[
                pl.BlockSpec((tok_rows // halves, tile), lambda n, info: (0, n))
                for _ in range(halves)
            ],
            scratch_shapes=[
                pltpu.VMEM((tok_rows, width), jnp.bfloat16),
                pltpu.VMEM((tok_rows, tile), jnp.float32),
            ],
        ),
        out_shape=[
            jax.ShapeDtypeStruct((tok_rows // halves, ff_local), dtype) for _ in range(halves)
        ],
        compiler_params=pltpu.CompilerParams(vmem_limit_bytes=VMEM_BYTES),
        name="partial_sums",
    )(info, units, weight, factors, *[first] * capacity)


def finish_kernel(own, left, right, gate, up, *rest):
    d_gate, d_up = rest[-2:]
    d_hidden = own[...] + left[...].astype(jnp.float32) + right[...].astype(jnp.float32)
    gate_float = gate[...].astype(jnp.float32)
    up_float = up[...].astype(jnp.float32)
    squash = jax.nn.sigmoid(gate_float)
    d_gate[...] = (d_hidden * up_float * squash * (1.0 + gate_float * (1.0 - squash))).astype(
        d_gate.dtype
    )
    d_up[...] = (d_hidden * (gate_float * squash)).astype(d_up.dtype)


def finish(own, left, right, gate, up, part, earlier):
    rows, ff_local = own.shape
    step = 128 if rows % 128 == 0 else rows
    steps = rows // step
    here = pl.BlockSpec((step, ff_local), lambda i: (i, 0))
    there = pl.BlockSpec((step, ff_local), lambda i: (part * steps + i, 0))
    before = [] if earlier is None else list(earlier)
    return pl.pallas_call(
        finish_kernel,
        grid=(steps,),
        in_specs=[here, here, here, there, there] + [pl.BlockSpec(memory_space=pl.ANY)] * len(before),
        out_specs=[there, there],
        out_shape=[jax.ShapeDtypeStruct(gate.shape, gate.dtype) for _ in range(2)],
        input_output_aliases={5: 0, 6: 1} if before else {},
        compiler_params=pltpu.CompilerParams(vmem_limit_bytes=VMEM_BYTES),
        name="finish",
    )(own, left, right, gate, up, *before)


def shards(
    output_gradient,
    saved_gate_value,
    saved_up_value,
    down_weight,
    adapter_first_weight,
    adapter_second_weight,
    adapter_of_block,
    slot_of_adapter,
):
    groups = lax.axis_size("dp")
    members = lax.axis_size("mp")
    my_group = lax.axis_index("dp")
    tok_rows = output_gradient.shape[0]
    blocks = tok_rows // BLK
    owner_totals = adapter_first_weight.shape[0]
    adapters = slot_of_adapter.shape[0]
    ff_local = saved_gate_value.shape[1]
    d_local = output_gradient.shape[1]
    capacity = (blocks + groups - 1) // groups
    halves = 1

    match_table = adapter_of_block[:, None] == jnp.arange(adapters, dtype=jnp.int32)[None, :]
    slot_of_block = jnp.sum(jnp.where(match_table, slot_of_adapter[None, :], 0), axis=1)
    owners = (slot_of_block // owner_totals).reshape(groups, blocks)
    local_slot = (slot_of_block % owner_totals).reshape(groups, blocks)
    block_index = jnp.arange(blocks, dtype=jnp.int32)
    earlier = (owners[:, :, None] == owners[:, None, :]) & (
        block_index[None, None, :] < block_index[None, :, None]
    )
    ranks = jnp.sum(earlier.astype(jnp.int32), axis=2)
    rank_values = jnp.arange(capacity, dtype=jnp.int32)
    hits = (owners == my_group)[:, None, :] & (ranks[:, None, :] == rank_values[None, :, None])
    incoming_valid = jnp.any(hits, axis=2)
    arriving_slot = jnp.sum(jnp.where(hits, local_slot[:, None, :], 0), axis=2)
    own_owner = lax.dynamic_index_in_dim(owners, my_group, 0, keepdims=False)
    own_rank = lax.dynamic_index_in_dim(ranks, my_group, 0, keepdims=False)
    group_values = jnp.arange(groups, dtype=jnp.int32)
    route_table = (own_owner[None, None, :] == group_values[:, None, None]) & (
        own_rank[None, None, :] == rank_values[None, :, None]
    )
    route_block = jnp.sum(jnp.where(route_table, block_index[None, None, :], 0), axis=2)

    moved, by_units = slices_of_tokens(output_gradient, groups, members, capacity * BLK)
    order = jnp.arange(groups, dtype=jnp.int32)
    origin = (my_group ^ order) if by_units else order
    place = origin
    routes = jnp.take(route_block, origin, axis=0)
    send_o = pack(routes, output_gradient)
    send_h = pack(routes, saved_gate_value, saved_up_value)
    slots = jnp.take(arriving_slot, origin, axis=0)
    valid = jnp.take(incoming_valid, origin, axis=0)
    last = groups - 1

    def target_of(reach, side):
        right = jnp.minimum(my_group + reach, last)
        left = jnp.maximum(my_group - reach, 0)
        if side:
            return right if side > 0 else left
        return jnp.where(my_group + reach <= last, right, left)

    def unit_of(group):
        unit = lax.dynamic_index_in_dim(moved, group, 0, keepdims=False)
        return unit.reshape(-1, d_local)

    if by_units:
        recv_o = send_o[:1] + [swap_over_dp(send_o[j], j) for j in range(1, groups)]
        recv_o, moved = lax.optimization_barrier((recv_o, moved))
        far = swap_over_dp(
            jnp.concatenate([send_h[3], unit_of(target_of(3, 0))], axis=1), 3, (0, 3)
        )
        far_h, far = far[:, :ff_local], far[:, ff_local:]
    else:
        recv_o, recv_h = all_to_all_of(send_o), all_to_all_of(send_h)
        units = lax.all_to_all(moved[:, 0], "dp", split_axis=0, concat_axis=0, tiled=True)
        others = lax.all_gather(units, "mp", axis=1, tiled=True)[None, :, None]

    def by_block(factor):
        return factor.reshape(groups, capacity, BLK, ADAPTER_RANK).astype(jnp.bfloat16)

    back_factor = by_block(
        adapter_scale * sum_over_mp(factor_parts(recv_o, adapter_second_weight, slots))
    )
    if by_units:
        far, back_factor, moved = lax.optimization_barrier((far, back_factor, moved))

        def gathered(*units):
            return lax.all_gather(
                jnp.stack([u.reshape(moved.shape[1:]) for u in units]), "mp", axis=0
            )

        far = gathered(far)
        pairs = [(i, i + 2) for i in range(groups - 2)] + [(i + 2, i) for i in range(groups - 2)]
        others = [
            lax.ppermute(unit_of(target_of(2, 0)), "dp", pairs),
            lax.ppermute(unit_of(target_of(1, -1)), "dp", [(i + 1, i) for i in range(last)]),
            lax.ppermute(unit_of(target_of(1, 1)), "dp", [(i, i + 1) for i in range(last)]),
        ]
        send_h[1], back_factor = lax.optimization_barrier((send_h[1], back_factor))
        recv_h = [send_h[0], swap_over_dp(send_h[1], 1), None, None]
        others, recv_h[1], back_factor = lax.optimization_barrier((others, recv_h[1], back_factor))
        others, _ = lax.optimization_barrier((others, far))
        others = gathered(*others, unit_of(my_group))

    table = jnp.stack(
        [
            incoming_valid.astype(jnp.int32),
            jnp.sum(jnp.where(hits, block_index, 0), axis=2),
            arriving_slot,
        ],
        axis=2,
    ).reshape(groups, 3 * capacity)
    table = jnp.concatenate([place[:, None], table], axis=1).astype(jnp.int32)

    def partial_for(target, reach, side, dtype=jnp.bfloat16):
        if not by_units:
            source, unit = others, target
        elif reach == 3:
            source, unit = far, 0
        else:
            source, unit = others, {2: 0, 1: 1 if side > 0 else 2, 0: 3}[reach]
        info = lax.dynamic_index_in_dim(table, target, 0, keepdims=False)
        info = jnp.concatenate([jnp.full((1,), unit, jnp.int32), info])
        return partial_sums(
            info, source, down_weight, back_factor, adapter_first_weight, tok_rows, halves, dtype
        )

    def joined(a, *more):
        total = a.astype(jnp.float32)
        for m in more:
            total = total + m.astype(jnp.float32)
        return total.astype(jnp.bfloat16)

    from_left = from_right = None
    for step in range(1, groups):
        reach = groups - step
        pairs_r = [(i, i + 1) for i in range(step)]
        pairs_l = [(last - i, last - 1 - i) for i in range(step)]
        if step <= reach:
            part = partial_for(target_of(reach, 0), reach, 0)
            if step > 1:
                came = [from_left] if from_right is None else [from_left, from_right]
                part = [joined(*each) for each in zip(part, *came)]
            send_r = send_l = part
            if step == last // 2 + 1 or not by_units:
                recv_h, send_r = lax.optimization_barrier((recv_h, send_r))
                send_l = send_r
                down_factor = by_block(
                    sum_over_mp(factor_parts(recv_h, adapter_first_weight, slots))
                )
        else:
            send_r = [joined(p, a) for p, a in zip(partial_for(target_of(reach, 1), reach, 1), from_left)]
            send_l = [joined(p, a) for p, a in zip(partial_for(target_of(reach, -1), reach, -1), from_right)]
        if by_units and step == last:
            send_r, send_l, late_h, late_o, late_factor = lax.optimization_barrier(
                (send_r, send_l, recv_h, recv_o, back_factor)
            )
            late_factor, down_factor = lax.optimization_barrier((late_factor, down_factor))
        if step < reach:
            from_left = [lax.ppermute(s, "dp", pairs_r + pairs_l) for s in send_r]
            from_right = None
            if by_units:
                middle_h = swap_over_dp(send_h[3], 3, (1, 2))
                recv_h[3] = jnp.where((my_group == 0) | (my_group == last), far_h, middle_h)
                recv_h[2] = swap_over_dp(send_h[2], 2)
        else:
            from_left = [lax.ppermute(s, "dp", pairs_r) for s in send_r]
            from_right = [lax.ppermute(s, "dp", pairs_l) for s in send_l]
    if by_units:
        recv_h, recv_o, back_factor = late_h, late_o, late_factor
    own = partial_for(my_group, 0, 0, jnp.float32)
    done = None
    for h in range(halves):
        done = finish(
            own[h], from_left[h], from_right[h], saved_gate_value, saved_up_value, h, done
        )
    d_gate, d_up = done

    def pieces(factor, packets):
        return jnp.stack(
            [
                jnp.einsum(
                    "ctr,ctf->crf",
                    factor[j],
                    packets[j].reshape(capacity, BLK, -1),
                    preferred_element_type=jnp.float32,
                )
                for j in range(groups)
            ]
        )

    terms_a = pieces(back_factor, recv_h).astype(jnp.bfloat16)
    terms_b = (adapter_scale * pieces(down_factor, recv_o)).astype(jnp.bfloat16)
    flat_slot = slots.reshape(groups * capacity)
    flat_valid = valid.reshape(groups * capacity)
    selector = (
        (flat_slot[None, :] == jnp.arange(owner_totals, dtype=jnp.int32)[:, None])
        & flat_valid[None, :]
    ).astype(jnp.bfloat16)
    grad_a = jnp.dot(
        selector,
        terms_a.reshape(groups * capacity, ADAPTER_RANK * ff_local),
        preferred_element_type=jnp.float32,
    ).reshape(owner_totals, ADAPTER_RANK, ff_local)
    grad_b = jnp.dot(
        selector,
        terms_b.reshape(groups * capacity, ADAPTER_RANK * d_local),
        preferred_element_type=jnp.float32,
    ).reshape(owner_totals, ADAPTER_RANK, d_local)
    return (d_gate, d_up, grad_a, grad_b)


def solution(mesh):
    in_specs = (
        P("dp", "mp"),
        P("dp", "mp"),
        P("dp", "mp"),
        P("mp", "dp"),
        P("dp", None, "mp"),
        P("dp", None, "mp"),
        P(),
        P(),
    )
    out_specs = (P("dp", "mp"), P("dp", "mp"), P("dp", None, "mp"), P("dp", None, "mp"))
    return jax.shard_map(shards, mesh=mesh, in_specs=in_specs, out_specs=out_specs, check_vma=False)
```

```python
import functools

import jax
import jax.numpy as jnp
from jax import lax
from jax.experimental import pallas as pl
from jax.experimental.pallas import tpu as pltpu
from jax.sharding import PartitionSpec as P

ADAPTER_RANK = 64
BLK = 64
VMEM_BYTES = 48 * 1024 * 1024


adapter_scale = 2.0


def sum_over_mp(x):
    size = lax.axis_size("mp")
    if size & (size - 1):
        return lax.psum(x, "mp")
    bit = 1
    while bit < size:
        x = x + lax.ppermute(x, "mp", [(i, i ^ bit) for i in range(size)])
        bit *= 2
    return x


def pack_kernel(count, capacity, info, *refs):
    sources, packets = refs[:-count], refs[-count:]
    step = pl.program_id(0)
    if len(sources) == capacity:
        values = [source[...] for source in sources]
    else:
        values = []
        for c in range(capacity):
            gate = sources[c][...].astype(jnp.float32)
            up = sources[capacity + c][...].astype(jnp.float32)
            values.append((gate * jax.nn.sigmoid(gate) * up).astype(jnp.bfloat16))
    for j in range(count):

        @pl.when(step == j)
        def _():
            for c in range(capacity):
                packets[j][c * BLK : (c + 1) * BLK, :] = values[c]


def pack(route, *sources):
    count, capacity = route.shape
    width = sources[0].shape[1]
    spec = [
        pl.BlockSpec((BLK, width), lambda i, info, c=c: (info[i * capacity + c], 0))
        for c in range(capacity)
    ]
    packets = pl.pallas_call(
        functools.partial(pack_kernel, count, capacity),
        grid_spec=pltpu.PrefetchScalarGridSpec(
            num_scalar_prefetch=1,
            grid=(count,),
            in_specs=spec * len(sources),
            out_specs=[
                pl.BlockSpec((capacity * BLK, width), lambda i, info: (0, 0)) for _ in range(count)
            ],
        ),
        out_shape=[jax.ShapeDtypeStruct((capacity * BLK, width), sources[0].dtype)] * count,
        compiler_params=pltpu.CompilerParams(vmem_limit_bytes=VMEM_BYTES),
        name="pack",
    )(route.reshape(-1), *[s for s in sources for _ in range(capacity)])
    return list(packets)


def all_to_all_of(parts):
    got = lax.all_to_all(jnp.stack(parts), "dp", split_axis=0, concat_axis=0, tiled=True)
    return [got[g] for g in range(len(parts))]


def swap_over_dp(x, bits, only=None):
    size = lax.axis_size("dp")
    return lax.ppermute(x, "dp", [(i, i ^ bits) for i in range(size) if only is None or i in only])


def factor_kernel(capacity, slots, *refs):
    weights, packets, result = refs[:capacity], refs[capacity:-1], refs[-1]
    step = pl.program_id(0)
    for j, packet in enumerate(packets):

        @pl.when(step == j)
        def _():
            for c in range(capacity):
                result[c] = lax.dot_general(
                    packet[c * BLK : (c + 1) * BLK, :],
                    weights[c][0],
                    (((1,), (1,)), ((), ())),
                    preferred_element_type=jnp.float32,
                )


def factor_parts(packets, weight, slots):
    count, capacity = slots.shape
    rank, width = weight.shape[1:]
    return pl.pallas_call(
        functools.partial(factor_kernel, capacity),
        grid_spec=pltpu.PrefetchScalarGridSpec(
            num_scalar_prefetch=1,
            grid=(count,),
            in_specs=[
                pl.BlockSpec((1, rank, width), lambda i, slots, c=c: (slots[i * capacity + c], 0, 0))
                for c in range(capacity)
            ]
            + [pl.BlockSpec((capacity * BLK, width), lambda i, slots: (0, 0)) for _ in packets],
            out_specs=pl.BlockSpec((capacity, BLK, rank), lambda i, slots: (i, 0, 0)),
        ),
        out_shape=jax.ShapeDtypeStruct((count * capacity, BLK, rank), jnp.float32),
        compiler_params=pltpu.CompilerParams(vmem_limit_bytes=VMEM_BYTES),
        name="factor_parts",
    )(slots.reshape(-1), *[weight] * capacity, *packets)


def slices_of_tokens(out, groups, members, block_rows):
    tok_rows, d_local = out.shape
    share = tok_rows // members
    moved = lax.all_to_all(
        out.reshape(members, share, d_local), "mp", split_axis=0, concat_axis=0, tiled=True
    )
    if members % groups or share % 16 or groups != 4 or tok_rows // groups != block_rows:
        moved = moved.transpose(1, 0, 2).reshape(share, groups, -1).transpose(1, 0, 2)
        return moved[:, None], False
    return moved.reshape(groups, members // groups, share, d_local), True


def partial_kernel(capacity, info, units_ref, w_ref, factor_ref, *rest):
    a_refs, outs, rows_ref, total_ref = rest[:capacity], rest[capacity:-2], rest[-2], rest[-1]

    @pl.when(pl.program_id(0) == 0)
    def _():
        members, _, parts, rows, columns = units_ref.shape
        for m in range(members):
            for q in range(parts):
                rows_ref[m * rows : (m + 1) * rows, q * columns : (q + 1) * columns] = units_ref[
                    m, 0, q
                ]

    total_ref[...] = lax.dot_general(
        rows_ref[...], w_ref[...], (((1,), (1,)), ((), ())), preferred_element_type=jnp.float32
    )
    for c in range(capacity):

        @pl.when(info[2 + 3 * c] > 0)
        def _():
            rows = pl.ds(pl.multiple_of(info[3 + 3 * c] * BLK, BLK), BLK)
            total_ref[rows, :] += jnp.dot(
                factor_ref[0, c], a_refs[c][0], preferred_element_type=jnp.float32
            )

    half = outs[0].shape[0]
    for h, out in enumerate(outs):
        out[...] = total_ref[h * half : (h + 1) * half, :].astype(out.dtype)


def partial_sums(info, units, weight, factors, first, tok_rows, halves, dtype):
    ff_local, width = weight.shape
    capacity, _, rank = factors.shape[1:]
    tile = 256 if ff_local % 256 == 0 else ff_local
    members, _, parts, rows, columns = units.shape
    return pl.pallas_call(
        functools.partial(partial_kernel, capacity),
        grid_spec=pltpu.PrefetchScalarGridSpec(
            num_scalar_prefetch=1,
            grid=(ff_local // tile,),
            in_specs=[
                pl.BlockSpec(
                    (members, 1, parts, rows, columns), lambda n, info: (0, info[0], 0, 0, 0)
                ),
                pl.BlockSpec((tile, width), lambda n, info: (n, 0)),
                pl.BlockSpec((1, capacity, BLK, rank), lambda n, info: (info[1], 0, 0, 0)),
            ]
            + [
                pl.BlockSpec((1, rank, tile), lambda n, info, c=c: (info[4 + 3 * c], 0, n))
                for c in range(capacity)
            ],
            out_specs=[
                pl.BlockSpec((tok_rows // halves, tile), lambda n, info: (0, n))
                for _ in range(halves)
            ],
            scratch_shapes=[
                pltpu.VMEM((tok_rows, width), jnp.bfloat16),
                pltpu.VMEM((tok_rows, tile), jnp.float32),
            ],
        ),
        out_shape=[
            jax.ShapeDtypeStruct((tok_rows // halves, ff_local), dtype) for _ in range(halves)
        ],
        compiler_params=pltpu.CompilerParams(vmem_limit_bytes=VMEM_BYTES),
        name="partial_sums",
    )(info, units, weight, factors, *[first] * capacity)


def finish_kernel(own, left, right, gate, up, *rest):
    d_gate, d_up = rest[-2:]
    d_hidden = own[...].astype(jnp.float32) + left[...].astype(jnp.float32)
    d_hidden += right[...].astype(jnp.float32)
    gate_float = gate[...].astype(jnp.float32)
    up_float = up[...].astype(jnp.float32)
    squash = jax.nn.sigmoid(gate_float)
    activated = gate_float * squash
    slope = squash + activated * (1.0 - squash)
    d_gate[...] = (d_hidden * up_float * slope).astype(d_gate.dtype)
    d_up[...] = (d_hidden * activated).astype(d_up.dtype)


def finish(own, left, right, gate, up, part, earlier):
    rows, ff_local = own.shape
    step = 128 if rows % 128 == 0 else rows
    steps = rows // step
    here = pl.BlockSpec((step, ff_local), lambda i: (i, 0))
    there = pl.BlockSpec((step, ff_local), lambda i: (part * steps + i, 0))
    before = [] if earlier is None else list(earlier)
    return pl.pallas_call(
        finish_kernel,
        grid=(steps,),
        in_specs=[here, here, here, there, there] + [pl.BlockSpec(memory_space=pl.ANY)] * len(before),
        out_specs=[there, there],
        out_shape=[jax.ShapeDtypeStruct(gate.shape, gate.dtype) for _ in range(2)],
        input_output_aliases={5: 0, 6: 1} if before else {},
        compiler_params=pltpu.CompilerParams(vmem_limit_bytes=VMEM_BYTES),
        name="finish",
    )(own, left, right, gate, up, *before)


def shards(
    output_gradient,
    saved_gate_value,
    saved_up_value,
    down_weight,
    adapter_first_weight,
    adapter_second_weight,
    adapter_of_block,
    slot_of_adapter,
):
    groups = lax.axis_size("dp")
    members = lax.axis_size("mp")
    my_group = lax.axis_index("dp")
    tok_rows = output_gradient.shape[0]
    blocks = tok_rows // BLK
    owner_totals = adapter_first_weight.shape[0]
    adapters = slot_of_adapter.shape[0]
    ff_local = saved_gate_value.shape[1]
    d_local = output_gradient.shape[1]
    capacity = (blocks + groups - 1) // groups
    halves = 1

    match_table = adapter_of_block[:, None] == jnp.arange(adapters, dtype=jnp.int32)[None, :]
    slot_of_block = jnp.sum(jnp.where(match_table, slot_of_adapter[None, :], 0), axis=1)
    owners = (slot_of_block // owner_totals).reshape(groups, blocks)
    local_slot = (slot_of_block % owner_totals).reshape(groups, blocks)
    block_index = jnp.arange(blocks, dtype=jnp.int32)
    earlier = (owners[:, :, None] == owners[:, None, :]) & (
        block_index[None, None, :] < block_index[None, :, None]
    )
    ranks = jnp.sum(earlier.astype(jnp.int32), axis=2)
    rank_values = jnp.arange(capacity, dtype=jnp.int32)
    hits = (owners == my_group)[:, None, :] & (ranks[:, None, :] == rank_values[None, :, None])
    incoming_valid = jnp.any(hits, axis=2)
    arriving_slot = jnp.sum(jnp.where(hits, local_slot[:, None, :], 0), axis=2)
    own_owner = lax.dynamic_index_in_dim(owners, my_group, 0, keepdims=False)
    own_rank = lax.dynamic_index_in_dim(ranks, my_group, 0, keepdims=False)
    group_values = jnp.arange(groups, dtype=jnp.int32)
    route_table = (own_owner[None, None, :] == group_values[:, None, None]) & (
        own_rank[None, None, :] == rank_values[None, :, None]
    )
    route_block = jnp.sum(jnp.where(route_table, block_index[None, None, :], 0), axis=2)

    moved, by_units = slices_of_tokens(output_gradient, groups, members, capacity * BLK)
    order = jnp.arange(groups, dtype=jnp.int32)
    origin = (my_group ^ order) if by_units else order
    place = origin
    routes = jnp.take(route_block, origin, axis=0)
    send_o = pack(routes, output_gradient)
    send_h = pack(routes, saved_gate_value, saved_up_value)
    slots = jnp.take(arriving_slot, origin, axis=0)
    valid = jnp.take(incoming_valid, origin, axis=0)
    last = groups - 1

    def target_of(reach, side):
        right = jnp.minimum(my_group + reach, last)
        left = jnp.maximum(my_group - reach, 0)
        if side:
            return right if side > 0 else left
        return jnp.where(my_group + reach <= last, right, left)

    def unit_of(group):
        unit = lax.dynamic_index_in_dim(moved, group, 0, keepdims=False)
        return unit.reshape(-1, d_local)

    if by_units:
        recv_o = send_o[:1] + [swap_over_dp(send_o[j], j) for j in range(1, groups)]
        far = swap_over_dp(unit_of(target_of(3, 0)), 3, (0, 3))
        recv_o, far, send_h[3] = lax.optimization_barrier((recv_o, far, send_h[3]))
        far_h = swap_over_dp(send_h[3], 3, (0, 3))
    else:
        recv_o, recv_h = all_to_all_of(send_o), all_to_all_of(send_h)
        units = lax.all_to_all(moved[:, 0], "dp", split_axis=0, concat_axis=0, tiled=True)
        others = lax.all_gather(units, "mp", axis=1, tiled=True)[None, :, None]

    def by_block(factor):
        return factor.reshape(groups, capacity, BLK, ADAPTER_RANK).astype(jnp.bfloat16)

    back_factor = by_block(
        adapter_scale * sum_over_mp(factor_parts(recv_o, adapter_second_weight, slots))
    )
    if by_units:
        far, far_h, back_factor, moved = lax.optimization_barrier((far, far_h, back_factor, moved))

        def gathered(*units):
            return lax.all_gather(
                jnp.stack([u.reshape(moved.shape[1:]) for u in units]), "mp", axis=0
            )

        far = gathered(far)
        pairs = [(i, i + 2) for i in range(groups - 2)] + [(i + 2, i) for i in range(groups - 2)]
        others = [
            lax.ppermute(unit_of(target_of(2, 0)), "dp", pairs),
            lax.ppermute(unit_of(target_of(1, -1)), "dp", [(i + 1, i) for i in range(last)]),
            lax.ppermute(unit_of(target_of(1, 1)), "dp", [(i, i + 1) for i in range(last)]),
        ]
        send_h[1], back_factor = lax.optimization_barrier((send_h[1], back_factor))
        recv_h = [send_h[0], swap_over_dp(send_h[1], 1), None, None]
        others, recv_h[1], back_factor = lax.optimization_barrier((others, recv_h[1], back_factor))
        others, _ = lax.optimization_barrier((others, far))
        others = gathered(*others, unit_of(my_group))

    table = jnp.stack(
        [
            incoming_valid.astype(jnp.int32),
            jnp.sum(jnp.where(hits, block_index, 0), axis=2),
            arriving_slot,
        ],
        axis=2,
    ).reshape(groups, 3 * capacity)
    table = jnp.concatenate([place[:, None], table], axis=1).astype(jnp.int32)

    def partial_for(target, reach, side, dtype=jnp.bfloat16):
        if not by_units:
            source, unit = others, target
        elif reach == 3:
            source, unit = far, 0
        else:
            source, unit = others, {2: 0, 1: 1 if side > 0 else 2, 0: 3}[reach]
        info = lax.dynamic_index_in_dim(table, target, 0, keepdims=False)
        info = jnp.concatenate([jnp.full((1,), unit, jnp.int32), info])
        return partial_sums(
            info, source, down_weight, back_factor, adapter_first_weight, tok_rows, halves, dtype
        )

    def joined(a, *more):
        total = a.astype(jnp.float32)
        for m in more:
            total = total + m.astype(jnp.float32)
        return total.astype(jnp.bfloat16)

    from_left = from_right = None
    for step in range(1, groups):
        reach = groups - step
        pairs_r = [(i, i + 1) for i in range(step)]
        pairs_l = [(last - i, last - 1 - i) for i in range(step)]
        if step <= reach:
            part = partial_for(target_of(reach, 0), reach, 0)
            if step > 1:
                came = [from_left] if from_right is None else [from_left, from_right]
                part = [joined(*each) for each in zip(part, *came)]
            send_r = send_l = part
            if step == last // 2 + 1 or not by_units:
                recv_h, send_r = lax.optimization_barrier((recv_h, send_r))
                send_l = send_r
                down_factor = by_block(
                    sum_over_mp(factor_parts(recv_h, adapter_first_weight, slots))
                )
        else:
            send_r = [joined(p, a) for p, a in zip(partial_for(target_of(reach, 1), reach, 1), from_left)]
            send_l = [joined(p, a) for p, a in zip(partial_for(target_of(reach, -1), reach, -1), from_right)]
        if by_units and step == last:
            send_r, send_l, late_h, late_o, late_factor = lax.optimization_barrier(
                (send_r, send_l, recv_h, recv_o, back_factor)
            )
            late_factor, down_factor = lax.optimization_barrier((late_factor, down_factor))
        if step < reach:
            from_left = [lax.ppermute(s, "dp", pairs_r + pairs_l) for s in send_r]
            from_right = None
            if by_units:
                middle_h = swap_over_dp(send_h[3], 3, (1, 2))
                recv_h[3] = jnp.where((my_group == 0) | (my_group == last), far_h, middle_h)
                recv_h[2] = swap_over_dp(send_h[2], 2)
        else:
            from_left = [lax.ppermute(s, "dp", pairs_r) for s in send_r]
            from_right = [lax.ppermute(s, "dp", pairs_l) for s in send_l]
    if by_units:
        recv_h, recv_o, back_factor = late_h, late_o, late_factor
    own = partial_for(my_group, 0, 0)
    done = None
    for h in range(halves):
        done = finish(
            own[h], from_left[h], from_right[h], saved_gate_value, saved_up_value, h, done
        )
    d_gate, d_up = done

    def pieces(factor, packets):
        return jnp.stack(
            [
                jnp.einsum(
                    "ctr,ctf->crf",
                    factor[j],
                    packets[j].reshape(capacity, BLK, -1),
                    preferred_element_type=jnp.float32,
                )
                for j in range(groups)
            ]
        )

    terms_a = pieces(back_factor, recv_h).astype(jnp.bfloat16)
    terms_b = (adapter_scale * pieces(down_factor, recv_o)).astype(jnp.bfloat16)
    flat_slot = slots.reshape(groups * capacity)
    flat_valid = valid.reshape(groups * capacity)
    selector = (
        (flat_slot[None, :] == jnp.arange(owner_totals, dtype=jnp.int32)[:, None])
        & flat_valid[None, :]
    ).astype(jnp.bfloat16)
    grad_a = jnp.dot(
        selector,
        terms_a.reshape(groups * capacity, ADAPTER_RANK * ff_local),
        preferred_element_type=jnp.float32,
    ).reshape(owner_totals, ADAPTER_RANK, ff_local)
    grad_b = jnp.dot(
        selector,
        terms_b.reshape(groups * capacity, ADAPTER_RANK * d_local),
        preferred_element_type=jnp.float32,
    ).reshape(owner_totals, ADAPTER_RANK, d_local)
    return (d_gate, d_up, grad_a, grad_b)


def solution(mesh):
    in_specs = (
        P("dp", "mp"),
        P("dp", "mp"),
        P("dp", "mp"),
        P("mp", "dp"),
        P("dp", None, "mp"),
        P("dp", None, "mp"),
        P(),
        P(),
    )
    out_specs = (P("dp", "mp"), P("dp", "mp"), P("dp", None, "mp"), P("dp", None, "mp"))
    return jax.shard_map(shards, mesh=mesh, in_specs=in_specs, out_specs=out_specs, check_vma=False)
```

```python
import functools

import jax
import jax.numpy as jnp
from jax import lax
from jax.experimental import pallas as pl
from jax.experimental.pallas import tpu as pltpu
from jax.sharding import PartitionSpec as P

ADAPTER_RANK = 64
BLK = 64
VMEM_BYTES = 48 * 1024 * 1024


adapter_scale = 2.0


def sum_over_mp(x):
    size = lax.axis_size("mp")
    if size & (size - 1):
        return lax.psum(x, "mp")
    bit = 1
    while bit < size:
        x = x + lax.ppermute(x, "mp", [(i, i ^ bit) for i in range(size)])
        bit *= 2
    return x


def pack_kernel(count, capacity, info, *refs):
    sources, packets = refs[:-count], refs[-count:]
    step = pl.program_id(0)
    if len(sources) == capacity:
        values = [source[...] for source in sources]
    else:
        values = []
        for c in range(capacity):
            gate = sources[c][...].astype(jnp.float32)
            up = sources[capacity + c][...].astype(jnp.float32)
            values.append((gate * jax.nn.sigmoid(gate) * up).astype(jnp.bfloat16))
    for j in range(count):

        @pl.when(step == j)
        def _():
            for c in range(capacity):
                packets[j][c * BLK : (c + 1) * BLK, :] = values[c]


def pack(route, *sources):
    count, capacity = route.shape
    width = sources[0].shape[1]
    spec = [
        pl.BlockSpec((BLK, width), lambda i, info, c=c: (info[i * capacity + c], 0))
        for c in range(capacity)
    ]
    packets = pl.pallas_call(
        functools.partial(pack_kernel, count, capacity),
        grid_spec=pltpu.PrefetchScalarGridSpec(
            num_scalar_prefetch=1,
            grid=(count,),
            in_specs=spec * len(sources),
            out_specs=[
                pl.BlockSpec((capacity * BLK, width), lambda i, info: (0, 0)) for _ in range(count)
            ],
        ),
        out_shape=[jax.ShapeDtypeStruct((capacity * BLK, width), sources[0].dtype)] * count,
        compiler_params=pltpu.CompilerParams(vmem_limit_bytes=VMEM_BYTES),
        name="pack",
    )(route.reshape(-1), *[s for s in sources for _ in range(capacity)])
    return list(packets)


def all_to_all_of(parts):
    got = lax.all_to_all(jnp.stack(parts), "dp", split_axis=0, concat_axis=0, tiled=True)
    return [got[g] for g in range(len(parts))]


def swap_over_dp(x, bits, only=None):
    size = lax.axis_size("dp")
    return lax.ppermute(x, "dp", [(i, i ^ bits) for i in range(size) if only is None or i in only])


def factor_kernel(capacity, slots, *refs):
    weights, packets, result = refs[:capacity], refs[capacity:-1], refs[-1]
    step = pl.program_id(0)
    for j, packet in enumerate(packets):

        @pl.when(step == j)
        def _():
            for c in range(capacity):
                result[c] = lax.dot_general(
                    packet[c * BLK : (c + 1) * BLK, :],
                    weights[c][0],
                    (((1,), (1,)), ((), ())),
                    preferred_element_type=jnp.float32,
                )


def factor_parts(packets, weight, slots):
    count, capacity = slots.shape
    rank, width = weight.shape[1:]
    return pl.pallas_call(
        functools.partial(factor_kernel, capacity),
        grid_spec=pltpu.PrefetchScalarGridSpec(
            num_scalar_prefetch=1,
            grid=(count,),
            in_specs=[
                pl.BlockSpec((1, rank, width), lambda i, slots, c=c: (slots[i * capacity + c], 0, 0))
                for c in range(capacity)
            ]
            + [pl.BlockSpec((capacity * BLK, width), lambda i, slots: (0, 0)) for _ in packets],
            out_specs=pl.BlockSpec((capacity, BLK, rank), lambda i, slots: (i, 0, 0)),
        ),
        out_shape=jax.ShapeDtypeStruct((count * capacity, BLK, rank), jnp.float32),
        compiler_params=pltpu.CompilerParams(vmem_limit_bytes=VMEM_BYTES),
        name="factor_parts",
    )(slots.reshape(-1), *[weight] * capacity, *packets)


def slices_of_tokens(out, groups, members, block_rows):
    tok_rows, d_local = out.shape
    share = tok_rows // members
    moved = lax.all_to_all(
        out.reshape(members, share, d_local), "mp", split_axis=0, concat_axis=0, tiled=True
    )
    if members % groups or share % 16 or groups != 4 or tok_rows // groups != block_rows:
        moved = moved.transpose(1, 0, 2).reshape(share, groups, -1).transpose(1, 0, 2)
        return moved[:, None], False
    return moved.reshape(groups, members // groups, share, d_local), True


def partial_kernel(capacity, info, units_ref, w_ref, factor_ref, *rest):
    a_refs, outs, rows_ref, total_ref = rest[:capacity], rest[capacity:-2], rest[-2], rest[-1]

    @pl.when(pl.program_id(0) == 0)
    def _():
        members, _, parts, rows, columns = units_ref.shape
        for m in range(members):
            for q in range(parts):
                rows_ref[m * rows : (m + 1) * rows, q * columns : (q + 1) * columns] = units_ref[
                    m, 0, q
                ]

    total_ref[...] = lax.dot_general(
        rows_ref[...], w_ref[...], (((1,), (1,)), ((), ())), preferred_element_type=jnp.float32
    )
    for c in range(capacity):

        @pl.when(info[2 + 3 * c] > 0)
        def _():
            rows = pl.ds(pl.multiple_of(info[3 + 3 * c] * BLK, BLK), BLK)
            total_ref[rows, :] += jnp.dot(
                factor_ref[0, c], a_refs[c][0], preferred_element_type=jnp.float32
            )

    half = outs[0].shape[0]
    for h, out in enumerate(outs):
        out[...] = total_ref[h * half : (h + 1) * half, :].astype(out.dtype)


def partial_sums(info, units, weight, factors, first, tok_rows, halves, dtype):
    ff_local, width = weight.shape
    capacity, _, rank = factors.shape[1:]
    tile = 256 if ff_local % 256 == 0 else ff_local
    members, _, parts, rows, columns = units.shape
    return pl.pallas_call(
        functools.partial(partial_kernel, capacity),
        grid_spec=pltpu.PrefetchScalarGridSpec(
            num_scalar_prefetch=1,
            grid=(ff_local // tile,),
            in_specs=[
                pl.BlockSpec(
                    (members, 1, parts, rows, columns), lambda n, info: (0, info[0], 0, 0, 0)
                ),
                pl.BlockSpec((tile, width), lambda n, info: (n, 0)),
                pl.BlockSpec((1, capacity, BLK, rank), lambda n, info: (info[1], 0, 0, 0)),
            ]
            + [
                pl.BlockSpec((1, rank, tile), lambda n, info, c=c: (info[4 + 3 * c], 0, n))
                for c in range(capacity)
            ],
            out_specs=[
                pl.BlockSpec((tok_rows // halves, tile), lambda n, info: (0, n))
                for _ in range(halves)
            ],
            scratch_shapes=[
                pltpu.VMEM((tok_rows, width), jnp.bfloat16),
                pltpu.VMEM((tok_rows, tile), jnp.float32),
            ],
        ),
        out_shape=[
            jax.ShapeDtypeStruct((tok_rows // halves, ff_local), dtype) for _ in range(halves)
        ],
        compiler_params=pltpu.CompilerParams(vmem_limit_bytes=VMEM_BYTES),
        name="partial_sums",
    )(info, units, weight, factors, *[first] * capacity)


def finish_kernel(own, right, gate, up, *rest):
    d_gate, d_up = rest[-2:]
    d_hidden = own[...].astype(jnp.float32) + right[...].astype(jnp.float32)
    gate_float = gate[...].astype(jnp.float32)
    up_float = up[...].astype(jnp.float32)
    squash = jax.nn.sigmoid(gate_float)
    activated = gate_float * squash
    slope = squash + activated * (1.0 - squash)
    d_gate[...] = (d_hidden * up_float * slope).astype(d_gate.dtype)
    d_up[...] = (d_hidden * activated).astype(d_up.dtype)


def finish(own, right, gate, up, part, earlier):
    rows, ff_local = own.shape
    step = 128 if rows % 128 == 0 else rows
    steps = rows // step
    here = pl.BlockSpec((step, ff_local), lambda i: (i, 0))
    there = pl.BlockSpec((step, ff_local), lambda i: (part * steps + i, 0))
    before = [] if earlier is None else list(earlier)
    return pl.pallas_call(
        finish_kernel,
        grid=(steps,),
        in_specs=[here, here, there, there] + [pl.BlockSpec(memory_space=pl.ANY)] * len(before),
        out_specs=[there, there],
        out_shape=[jax.ShapeDtypeStruct(gate.shape, gate.dtype) for _ in range(2)],
        input_output_aliases={4: 0, 5: 1} if before else {},
        compiler_params=pltpu.CompilerParams(vmem_limit_bytes=VMEM_BYTES),
        name="finish",
    )(own, right, gate, up, *before)


def shards(
    output_gradient,
    saved_gate_value,
    saved_up_value,
    down_weight,
    adapter_first_weight,
    adapter_second_weight,
    adapter_of_block,
    slot_of_adapter,
):
    groups = lax.axis_size("dp")
    members = lax.axis_size("mp")
    my_group = lax.axis_index("dp")
    tok_rows = output_gradient.shape[0]
    blocks = tok_rows // BLK
    owner_totals = adapter_first_weight.shape[0]
    adapters = slot_of_adapter.shape[0]
    ff_local = saved_gate_value.shape[1]
    d_local = output_gradient.shape[1]
    capacity = (blocks + groups - 1) // groups
    halves = 1

    match_table = adapter_of_block[:, None] == jnp.arange(adapters, dtype=jnp.int32)[None, :]
    slot_of_block = jnp.sum(jnp.where(match_table, slot_of_adapter[None, :], 0), axis=1)
    owners = (slot_of_block // owner_totals).reshape(groups, blocks)
    local_slot = (slot_of_block % owner_totals).reshape(groups, blocks)
    block_index = jnp.arange(blocks, dtype=jnp.int32)
    earlier = (owners[:, :, None] == owners[:, None, :]) & (
        block_index[None, None, :] < block_index[None, :, None]
    )
    ranks = jnp.sum(earlier.astype(jnp.int32), axis=2)
    rank_values = jnp.arange(capacity, dtype=jnp.int32)
    hits = (owners == my_group)[:, None, :] & (ranks[:, None, :] == rank_values[None, :, None])
    incoming_valid = jnp.any(hits, axis=2)
    arriving_slot = jnp.sum(jnp.where(hits, local_slot[:, None, :], 0), axis=2)
    own_owner = lax.dynamic_index_in_dim(owners, my_group, 0, keepdims=False)
    own_rank = lax.dynamic_index_in_dim(ranks, my_group, 0, keepdims=False)
    group_values = jnp.arange(groups, dtype=jnp.int32)
    route_table = (own_owner[None, None, :] == group_values[:, None, None]) & (
        own_rank[None, None, :] == rank_values[None, :, None]
    )
    route_block = jnp.sum(jnp.where(route_table, block_index[None, None, :], 0), axis=2)

    moved, by_units = slices_of_tokens(output_gradient, groups, members, capacity * BLK)
    order = jnp.arange(groups, dtype=jnp.int32)
    origin = (my_group ^ order) if by_units else order
    place = origin
    routes = jnp.take(route_block, origin, axis=0)
    send_o = pack(routes, output_gradient)
    send_h = pack(routes, saved_gate_value, saved_up_value)
    slots = jnp.take(arriving_slot, origin, axis=0)
    valid = jnp.take(incoming_valid, origin, axis=0)
    last = groups - 1

    def target_of(reach, side):
        right = jnp.minimum(my_group + reach, last)
        left = jnp.maximum(my_group - reach, 0)
        if side:
            return right if side > 0 else left
        return jnp.where(my_group + reach <= last, right, left)

    def unit_of(group):
        unit = lax.dynamic_index_in_dim(moved, group, 0, keepdims=False)
        return unit.reshape(-1, d_local)

    if by_units:
        recv_o = send_o[:1] + [swap_over_dp(send_o[j], j) for j in range(1, groups)]
        far = swap_over_dp(unit_of(target_of(3, 0)), 3, (0, 3))
        recv_o, far, send_h[3] = lax.optimization_barrier((recv_o, far, send_h[3]))
        far_h = swap_over_dp(send_h[3], 3, (0, 3))
    else:
        recv_o, recv_h = all_to_all_of(send_o), all_to_all_of(send_h)
        units = lax.all_to_all(moved[:, 0], "dp", split_axis=0, concat_axis=0, tiled=True)
        others = lax.all_gather(units, "mp", axis=1, tiled=True)[None, :, None]

    def by_block(factor):
        return factor.reshape(groups, capacity, BLK, ADAPTER_RANK).astype(jnp.bfloat16)

    back_factor = by_block(
        adapter_scale * sum_over_mp(factor_parts(recv_o, adapter_second_weight, slots))
    )
    if by_units:
        far, far_h, back_factor, moved = lax.optimization_barrier((far, far_h, back_factor, moved))

        def gathered(*units):
            return lax.all_gather(
                jnp.stack([u.reshape(moved.shape[1:]) for u in units]), "mp", axis=0
            )

        far = gathered(far)
        pairs = [(i, i + 2) for i in range(groups - 2)] + [(i + 2, i) for i in range(groups - 2)]
        others = [
            lax.ppermute(unit_of(target_of(2, 0)), "dp", pairs),
            lax.ppermute(unit_of(target_of(1, -1)), "dp", [(i + 1, i) for i in range(last)]),
            lax.ppermute(unit_of(target_of(1, 1)), "dp", [(i, i + 1) for i in range(last)]),
        ]
        send_h[1], back_factor = lax.optimization_barrier((send_h[1], back_factor))
        recv_h = [send_h[0], swap_over_dp(send_h[1], 1), None, None]
        others, recv_h[1], back_factor = lax.optimization_barrier((others, recv_h[1], back_factor))
        others, _ = lax.optimization_barrier((others, far))
        others = gathered(*others, unit_of(my_group))

    table = jnp.stack(
        [
            incoming_valid.astype(jnp.int32),
            jnp.sum(jnp.where(hits, block_index, 0), axis=2),
            arriving_slot,
        ],
        axis=2,
    ).reshape(groups, 3 * capacity)
    table = jnp.concatenate([place[:, None], table], axis=1).astype(jnp.int32)

    def partial_for(target, reach, side, dtype=jnp.bfloat16):
        if not by_units:
            source, unit = others, target
        elif reach == 3:
            source, unit = far, 0
        else:
            source, unit = others, {2: 0, 1: 1 if side > 0 else 2, 0: 3}[reach]
        info = lax.dynamic_index_in_dim(table, target, 0, keepdims=False)
        info = jnp.concatenate([jnp.full((1,), unit, jnp.int32), info])
        return partial_sums(
            info, source, down_weight, back_factor, adapter_first_weight, tok_rows, halves, dtype
        )

    def joined(a, *more):
        total = a.astype(jnp.float32)
        for m in more:
            total = total + m.astype(jnp.float32)
        return total.astype(jnp.bfloat16)

    from_left = from_right = None
    for step in range(1, groups):
        reach = groups - step
        pairs_r = [(i, i + 1) for i in range(step)]
        pairs_l = [(last - i, last - 1 - i) for i in range(step)]
        if step <= reach:
            part = partial_for(target_of(reach, 0), reach, 0)
            if step > 1:
                came = [from_left] if from_right is None else [from_left, from_right]
                part = [joined(*each) for each in zip(part, *came)]
            send_r = send_l = part
            if step == last // 2 + 1 or not by_units:
                recv_h, send_r = lax.optimization_barrier((recv_h, send_r))
                send_l = send_r
                down_factor = by_block(
                    sum_over_mp(factor_parts(recv_h, adapter_first_weight, slots))
                )
        else:
            send_r = [joined(p, a) for p, a in zip(partial_for(target_of(reach, 1), reach, 1), from_left)]
            send_l = [joined(p, a) for p, a in zip(partial_for(target_of(reach, -1), reach, -1), from_right)]
        if by_units and step == last:
            send_r, send_l, late_h, late_o, late_factor = lax.optimization_barrier(
                (send_r, send_l, recv_h, recv_o, back_factor)
            )
            late_factor, down_factor = lax.optimization_barrier((late_factor, down_factor))
        if step < reach:
            from_left = [lax.ppermute(s, "dp", pairs_r + pairs_l) for s in send_r]
            from_right = None
            if by_units:
                middle_h = swap_over_dp(send_h[3], 3, (1, 2))
                recv_h[3] = jnp.where((my_group == 0) | (my_group == last), far_h, middle_h)
                recv_h[2] = swap_over_dp(send_h[2], 2)
        else:
            from_left = [lax.ppermute(s, "dp", pairs_r) for s in send_r]
            from_right = [lax.ppermute(s, "dp", pairs_l) for s in send_l]
    if by_units:
        recv_h, recv_o, back_factor = late_h, late_o, late_factor
    own = partial_for(my_group, 0, 0)
    done = None
    for h in range(halves):
        done = finish(
            joined(own[h], from_left[h]), from_right[h], saved_gate_value, saved_up_value, h, done
        )
    d_gate, d_up = done

    def pieces(factor, packets):
        return jnp.stack(
            [
                jnp.einsum(
                    "ctr,ctf->crf",
                    factor[j],
                    packets[j].reshape(capacity, BLK, -1),
                    preferred_element_type=jnp.float32,
                )
                for j in range(groups)
            ]
        )

    terms_a = pieces(back_factor, recv_h).astype(jnp.bfloat16)
    terms_b = (adapter_scale * pieces(down_factor, recv_o)).astype(jnp.bfloat16)
    flat_slot = slots.reshape(groups * capacity)
    flat_valid = valid.reshape(groups * capacity)
    selector = (
        (flat_slot[None, :] == jnp.arange(owner_totals, dtype=jnp.int32)[:, None])
        & flat_valid[None, :]
    ).astype(jnp.bfloat16)
    grad_a = jnp.dot(
        selector,
        terms_a.reshape(groups * capacity, ADAPTER_RANK * ff_local),
        preferred_element_type=jnp.float32,
    ).reshape(owner_totals, ADAPTER_RANK, ff_local)
    grad_b = jnp.dot(
        selector,
        terms_b.reshape(groups * capacity, ADAPTER_RANK * d_local),
        preferred_element_type=jnp.float32,
    ).reshape(owner_totals, ADAPTER_RANK, d_local)
    return (d_gate, d_up, grad_a, grad_b)


def solution(mesh):
    in_specs = (
        P("dp", "mp"),
        P("dp", "mp"),
        P("dp", "mp"),
        P("mp", "dp"),
        P("dp", None, "mp"),
        P("dp", None, "mp"),
        P(),
        P(),
    )
    out_specs = (P("dp", "mp"), P("dp", "mp"), P("dp", None, "mp"), P("dp", None, "mp"))
    return jax.shard_map(shards, mesh=mesh, in_specs=in_specs, out_specs=out_specs, check_vma=False)
```

```python
import functools

import jax
import jax.numpy as jnp
from jax import lax
from jax.experimental import pallas as pl
from jax.experimental.pallas import tpu as pltpu
from jax.sharding import PartitionSpec as P

ADAPTER_RANK = 64
BLK = 64
VMEM_BYTES = 48 * 1024 * 1024


adapter_scale = 2.0


def sum_over_mp(x):
    size = lax.axis_size("mp")
    if size & (size - 1):
        return lax.psum(x, "mp")
    bit = 1
    while bit < size:
        x = x + lax.ppermute(x, "mp", [(i, i ^ bit) for i in range(size)])
        bit *= 2
    return x


def pack_kernel(count, capacity, info, *refs):
    sources, packets = refs[:-count], refs[-count:]
    step = pl.program_id(0)
    if len(sources) == capacity:
        values = [source[...] for source in sources]
    else:
        values = []
        for c in range(capacity):
            gate = sources[c][...].astype(jnp.float32)
            up = sources[capacity + c][...].astype(jnp.float32)
            values.append((gate * jax.nn.sigmoid(gate) * up).astype(jnp.bfloat16))
    for j in range(count):

        @pl.when(step == j)
        def _():
            for c in range(capacity):
                packets[j][c * BLK : (c + 1) * BLK, :] = values[c]


def pack(route, *sources):
    count, capacity = route.shape
    width = sources[0].shape[1]
    spec = [
        pl.BlockSpec((BLK, width), lambda i, info, c=c: (info[i * capacity + c], 0))
        for c in range(capacity)
    ]
    packets = pl.pallas_call(
        functools.partial(pack_kernel, count, capacity),
        grid_spec=pltpu.PrefetchScalarGridSpec(
            num_scalar_prefetch=1,
            grid=(count,),
            in_specs=spec * len(sources),
            out_specs=[
                pl.BlockSpec((capacity * BLK, width), lambda i, info: (0, 0)) for _ in range(count)
            ],
        ),
        out_shape=[jax.ShapeDtypeStruct((capacity * BLK, width), sources[0].dtype)] * count,
        compiler_params=pltpu.CompilerParams(vmem_limit_bytes=VMEM_BYTES),
        name="pack",
    )(route.reshape(-1), *[s for s in sources for _ in range(capacity)])
    return list(packets)


def all_to_all_of(parts):
    got = lax.all_to_all(jnp.stack(parts), "dp", split_axis=0, concat_axis=0, tiled=True)
    return [got[g] for g in range(len(parts))]


def swap_over_dp(x, bits, only=None):
    size = lax.axis_size("dp")
    return lax.ppermute(x, "dp", [(i, i ^ bits) for i in range(size) if only is None or i in only])


def factor_kernel(capacity, slots, *refs):
    weights, packets, result = refs[:capacity], refs[capacity:-1], refs[-1]
    step = pl.program_id(0)
    for j, packet in enumerate(packets):

        @pl.when(step == j)
        def _():
            for c in range(capacity):
                result[c] = lax.dot_general(
                    packet[c * BLK : (c + 1) * BLK, :],
                    weights[c][0],
                    (((1,), (1,)), ((), ())),
                    preferred_element_type=jnp.float32,
                )


def factor_parts(packets, weight, slots):
    count, capacity = slots.shape
    rank, width = weight.shape[1:]
    return pl.pallas_call(
        functools.partial(factor_kernel, capacity),
        grid_spec=pltpu.PrefetchScalarGridSpec(
            num_scalar_prefetch=1,
            grid=(count,),
            in_specs=[
                pl.BlockSpec((1, rank, width), lambda i, slots, c=c: (slots[i * capacity + c], 0, 0))
                for c in range(capacity)
            ]
            + [pl.BlockSpec((capacity * BLK, width), lambda i, slots: (0, 0)) for _ in packets],
            out_specs=pl.BlockSpec((capacity, BLK, rank), lambda i, slots: (i, 0, 0)),
        ),
        out_shape=jax.ShapeDtypeStruct((count * capacity, BLK, rank), jnp.float32),
        compiler_params=pltpu.CompilerParams(vmem_limit_bytes=VMEM_BYTES),
        name="factor_parts",
    )(slots.reshape(-1), *[weight] * capacity, *packets)


def slices_of_tokens(out, groups, members, block_rows):
    tok_rows, d_local = out.shape
    share = tok_rows // members
    moved = lax.all_to_all(
        out.reshape(members, share, d_local), "mp", split_axis=0, concat_axis=0, tiled=True
    )
    if members % groups or share % 16 or groups != 4 or tok_rows // groups != block_rows:
        moved = moved.transpose(1, 0, 2).reshape(share, groups, -1).transpose(1, 0, 2)
        return moved[:, None], False
    return moved.reshape(groups, members // groups, share, d_local), True


def partial_kernel(capacity, info, units_ref, w_ref, factor_ref, *rest):
    a_refs, outs, rows_ref, total_ref = rest[:capacity], rest[capacity:-2], rest[-2], rest[-1]

    @pl.when(pl.program_id(0) == 0)
    def _():
        members, _, parts, rows, columns = units_ref.shape
        for m in range(members):
            for q in range(parts):
                rows_ref[m * rows : (m + 1) * rows, q * columns : (q + 1) * columns] = units_ref[
                    m, 0, q
                ]

    total_ref[...] = lax.dot_general(
        rows_ref[...], w_ref[...], (((1,), (1,)), ((), ())), preferred_element_type=jnp.float32
    )
    for c in range(capacity):

        @pl.when(info[2 + 3 * c] > 0)
        def _():
            rows = pl.ds(pl.multiple_of(info[3 + 3 * c] * BLK, BLK), BLK)
            total_ref[rows, :] += jnp.dot(
                factor_ref[0, c], a_refs[c][0], preferred_element_type=jnp.float32
            )

    half = outs[0].shape[0]
    for h, out in enumerate(outs):
        out[...] = total_ref[h * half : (h + 1) * half, :].astype(out.dtype)


def partial_sums(info, units, weight, factors, first, tok_rows, halves, dtype):
    ff_local, width = weight.shape
    capacity, _, rank = factors.shape[1:]
    tile = 256 if ff_local % 256 == 0 else ff_local
    members, _, parts, rows, columns = units.shape
    return pl.pallas_call(
        functools.partial(partial_kernel, capacity),
        grid_spec=pltpu.PrefetchScalarGridSpec(
            num_scalar_prefetch=1,
            grid=(ff_local // tile,),
            in_specs=[
                pl.BlockSpec(
                    (members, 1, parts, rows, columns), lambda n, info: (0, info[0], 0, 0, 0)
                ),
                pl.BlockSpec((tile, width), lambda n, info: (n, 0)),
                pl.BlockSpec((1, capacity, BLK, rank), lambda n, info: (info[1], 0, 0, 0)),
            ]
            + [
                pl.BlockSpec((1, rank, tile), lambda n, info, c=c: (info[4 + 3 * c], 0, n))
                for c in range(capacity)
            ],
            out_specs=[
                pl.BlockSpec((tok_rows // halves, tile), lambda n, info: (0, n))
                for _ in range(halves)
            ],
            scratch_shapes=[
                pltpu.VMEM((tok_rows, width), jnp.bfloat16),
                pltpu.VMEM((tok_rows, tile), jnp.float32),
            ],
        ),
        out_shape=[
            jax.ShapeDtypeStruct((tok_rows // halves, ff_local), dtype) for _ in range(halves)
        ],
        compiler_params=pltpu.CompilerParams(vmem_limit_bytes=VMEM_BYTES),
        name="partial_sums",
    )(info, units, weight, factors, *[first] * capacity)


def finish_kernel(own, left, right, gate, up, *rest):
    d_gate, d_up = rest[-2:]
    d_hidden = own[...].astype(jnp.float32) + left[...].astype(jnp.float32)
    d_hidden += right[...].astype(jnp.float32)
    gate_float = gate[...].astype(jnp.float32)
    up_float = up[...].astype(jnp.float32)
    squash = jax.nn.sigmoid(gate_float)
    activated = gate_float * squash
    slope = squash + activated * (1.0 - squash)
    d_gate[...] = (d_hidden * up_float * slope).astype(d_gate.dtype)
    d_up[...] = (d_hidden * activated).astype(d_up.dtype)


def finish(own, left, right, gate, up, part, earlier):
    rows, ff_local = own.shape
    step = 64 if rows % 64 == 0 else rows
    steps = rows // step
    here = pl.BlockSpec((step, ff_local), lambda i: (i, 0))
    there = pl.BlockSpec((step, ff_local), lambda i: (part * steps + i, 0))
    before = [] if earlier is None else list(earlier)
    return pl.pallas_call(
        finish_kernel,
        grid=(steps,),
        in_specs=[here, here, here, there, there] + [pl.BlockSpec(memory_space=pl.ANY)] * len(before),
        out_specs=[there, there],
        out_shape=[jax.ShapeDtypeStruct(gate.shape, gate.dtype) for _ in range(2)],
        input_output_aliases={5: 0, 6: 1} if before else {},
        compiler_params=pltpu.CompilerParams(vmem_limit_bytes=VMEM_BYTES),
        name="finish",
    )(own, left, right, gate, up, *before)


def shards(
    output_gradient,
    saved_gate_value,
    saved_up_value,
    down_weight,
    adapter_first_weight,
    adapter_second_weight,
    adapter_of_block,
    slot_of_adapter,
):
    groups = lax.axis_size("dp")
    members = lax.axis_size("mp")
    my_group = lax.axis_index("dp")
    tok_rows = output_gradient.shape[0]
    blocks = tok_rows // BLK
    owner_totals = adapter_first_weight.shape[0]
    adapters = slot_of_adapter.shape[0]
    ff_local = saved_gate_value.shape[1]
    d_local = output_gradient.shape[1]
    capacity = (blocks + groups - 1) // groups
    halves = 1

    match_table = adapter_of_block[:, None] == jnp.arange(adapters, dtype=jnp.int32)[None, :]
    slot_of_block = jnp.sum(jnp.where(match_table, slot_of_adapter[None, :], 0), axis=1)
    owners = (slot_of_block // owner_totals).reshape(groups, blocks)
    local_slot = (slot_of_block % owner_totals).reshape(groups, blocks)
    block_index = jnp.arange(blocks, dtype=jnp.int32)
    earlier = (owners[:, :, None] == owners[:, None, :]) & (
        block_index[None, None, :] < block_index[None, :, None]
    )
    ranks = jnp.sum(earlier.astype(jnp.int32), axis=2)
    rank_values = jnp.arange(capacity, dtype=jnp.int32)
    hits = (owners == my_group)[:, None, :] & (ranks[:, None, :] == rank_values[None, :, None])
    incoming_valid = jnp.any(hits, axis=2)
    arriving_slot = jnp.sum(jnp.where(hits, local_slot[:, None, :], 0), axis=2)
    own_owner = lax.dynamic_index_in_dim(owners, my_group, 0, keepdims=False)
    own_rank = lax.dynamic_index_in_dim(ranks, my_group, 0, keepdims=False)
    group_values = jnp.arange(groups, dtype=jnp.int32)
    route_table = (own_owner[None, None, :] == group_values[:, None, None]) & (
        own_rank[None, None, :] == rank_values[None, :, None]
    )
    route_block = jnp.sum(jnp.where(route_table, block_index[None, None, :], 0), axis=2)

    moved, by_units = slices_of_tokens(output_gradient, groups, members, capacity * BLK)
    order = jnp.arange(groups, dtype=jnp.int32)
    origin = (my_group ^ order) if by_units else order
    place = origin
    routes = jnp.take(route_block, origin, axis=0)
    send_o = pack(routes, output_gradient)
    send_h = pack(routes, saved_gate_value, saved_up_value)
    slots = jnp.take(arriving_slot, origin, axis=0)
    valid = jnp.take(incoming_valid, origin, axis=0)
    last = groups - 1

    def target_of(reach, side):
        right = jnp.minimum(my_group + reach, last)
        left = jnp.maximum(my_group - reach, 0)
        if side:
            return right if side > 0 else left
        return jnp.where(my_group + reach <= last, right, left)

    def unit_of(group):
        unit = lax.dynamic_index_in_dim(moved, group, 0, keepdims=False)
        return unit.reshape(-1, d_local)

    if by_units:
        recv_o = send_o[:1] + [swap_over_dp(send_o[j], j) for j in range(1, groups)]
        far = swap_over_dp(unit_of(target_of(3, 0)), 3, (0, 3))
        recv_o, far, send_h[3] = lax.optimization_barrier((recv_o, far, send_h[3]))
        far_h = swap_over_dp(send_h[3], 3, (0, 3))
    else:
        recv_o, recv_h = all_to_all_of(send_o), all_to_all_of(send_h)
        units = lax.all_to_all(moved[:, 0], "dp", split_axis=0, concat_axis=0, tiled=True)
        others = lax.all_gather(units, "mp", axis=1, tiled=True)[None, :, None]

    def by_block(factor):
        return factor.reshape(groups, capacity, BLK, ADAPTER_RANK).astype(jnp.bfloat16)

    back_factor = by_block(
        adapter_scale * sum_over_mp(factor_parts(recv_o, adapter_second_weight, slots))
    )
    if by_units:
        far, far_h, back_factor, moved = lax.optimization_barrier((far, far_h, back_factor, moved))

        def gathered(*units):
            return lax.all_gather(
                jnp.stack([u.reshape(moved.shape[1:]) for u in units]), "mp", axis=0
            )

        far = gathered(far)
        pairs = [(i, i + 2) for i in range(groups - 2)] + [(i + 2, i) for i in range(groups - 2)]
        others = [
            lax.ppermute(unit_of(target_of(2, 0)), "dp", pairs),
            lax.ppermute(unit_of(target_of(1, -1)), "dp", [(i + 1, i) for i in range(last)]),
            lax.ppermute(unit_of(target_of(1, 1)), "dp", [(i, i + 1) for i in range(last)]),
        ]
        send_h[1], back_factor = lax.optimization_barrier((send_h[1], back_factor))
        recv_h = [send_h[0], swap_over_dp(send_h[1], 1), None, None]
        others, recv_h[1], back_factor = lax.optimization_barrier((others, recv_h[1], back_factor))
        others, _ = lax.optimization_barrier((others, far))
        others = gathered(*others, unit_of(my_group))

    table = jnp.stack(
        [
            incoming_valid.astype(jnp.int32),
            jnp.sum(jnp.where(hits, block_index, 0), axis=2),
            arriving_slot,
        ],
        axis=2,
    ).reshape(groups, 3 * capacity)
    table = jnp.concatenate([place[:, None], table], axis=1).astype(jnp.int32)

    def partial_for(target, reach, side, dtype=jnp.bfloat16):
        if not by_units:
            source, unit = others, target
        elif reach == 3:
            source, unit = far, 0
        else:
            source, unit = others, {2: 0, 1: 1 if side > 0 else 2, 0: 3}[reach]
        info = lax.dynamic_index_in_dim(table, target, 0, keepdims=False)
        info = jnp.concatenate([jnp.full((1,), unit, jnp.int32), info])
        return partial_sums(
            info, source, down_weight, back_factor, adapter_first_weight, tok_rows, halves, dtype
        )

    def joined(a, *more):
        total = a.astype(jnp.float32)
        for m in more:
            total = total + m.astype(jnp.float32)
        return total.astype(jnp.bfloat16)

    from_left = from_right = None
    for step in range(1, groups):
        reach = groups - step
        pairs_r = [(i, i + 1) for i in range(step)]
        pairs_l = [(last - i, last - 1 - i) for i in range(step)]
        if step <= reach:
            part = partial_for(target_of(reach, 0), reach, 0)
            if step > 1:
                came = [from_left] if from_right is None else [from_left, from_right]
                part = [joined(*each) for each in zip(part, *came)]
            send_r = send_l = part
            if step == last // 2 + 1 or not by_units:
                recv_h, send_r = lax.optimization_barrier((recv_h, send_r))
                send_l = send_r
                down_factor = by_block(
                    sum_over_mp(factor_parts(recv_h, adapter_first_weight, slots))
                )
        else:
            send_r = [joined(p, a) for p, a in zip(partial_for(target_of(reach, 1), reach, 1), from_left)]
            send_l = [joined(p, a) for p, a in zip(partial_for(target_of(reach, -1), reach, -1), from_right)]
        if by_units and step == last:
            send_r, send_l, late_h, late_o, late_factor = lax.optimization_barrier(
                (send_r, send_l, recv_h, recv_o, back_factor)
            )
            late_factor, down_factor = lax.optimization_barrier((late_factor, down_factor))
        if step < reach:
            from_left = [lax.ppermute(s, "dp", pairs_r + pairs_l) for s in send_r]
            from_right = None
            if by_units:
                middle_h = swap_over_dp(send_h[3], 3, (1, 2))
                recv_h[3] = jnp.where((my_group == 0) | (my_group == last), far_h, middle_h)
                recv_h[2] = swap_over_dp(send_h[2], 2)
        else:
            from_left = [lax.ppermute(s, "dp", pairs_r) for s in send_r]
            from_right = [lax.ppermute(s, "dp", pairs_l) for s in send_l]
    if by_units:
        recv_h, recv_o, back_factor = late_h, late_o, late_factor
    own = partial_for(my_group, 0, 0)
    done = None
    for h in range(halves):
        done = finish(
            own[h], from_left[h], from_right[h], saved_gate_value, saved_up_value, h, done
        )
    d_gate, d_up = done

    def pieces(factor, packets):
        return jnp.stack(
            [
                jnp.einsum(
                    "ctr,ctf->crf",
                    factor[j],
                    packets[j].reshape(capacity, BLK, -1),
                    preferred_element_type=jnp.float32,
                )
                for j in range(groups)
            ]
        )

    terms_a = pieces(back_factor, recv_h).astype(jnp.bfloat16)
    terms_b = (adapter_scale * pieces(down_factor, recv_o)).astype(jnp.bfloat16)
    flat_slot = slots.reshape(groups * capacity)
    flat_valid = valid.reshape(groups * capacity)
    selector = (
        (flat_slot[None, :] == jnp.arange(owner_totals, dtype=jnp.int32)[:, None])
        & flat_valid[None, :]
    ).astype(jnp.bfloat16)
    grad_a = jnp.dot(
        selector,
        terms_a.reshape(groups * capacity, ADAPTER_RANK * ff_local),
        preferred_element_type=jnp.float32,
    ).reshape(owner_totals, ADAPTER_RANK, ff_local)
    grad_b = jnp.dot(
        selector,
        terms_b.reshape(groups * capacity, ADAPTER_RANK * d_local),
        preferred_element_type=jnp.float32,
    ).reshape(owner_totals, ADAPTER_RANK, d_local)
    return (d_gate, d_up, grad_a, grad_b)


def solution(mesh):
    in_specs = (
        P("dp", "mp"),
        P("dp", "mp"),
        P("dp", "mp"),
        P("mp", "dp"),
        P("dp", None, "mp"),
        P("dp", None, "mp"),
        P(),
        P(),
    )
    out_specs = (P("dp", "mp"), P("dp", "mp"), P("dp", None, "mp"), P("dp", None, "mp"))
    return jax.shard_map(shards, mesh=mesh, in_specs=in_specs, out_specs=out_specs, check_vma=False)
```
